256 devices in a mesh: view: 2 (over core), dp: 8 (over z), unit: 16 (over x, y).
Axes of the slice: x: 4, y: 4, z: 8, core: 2. Of those that a mesh axis runs over, the one named last changes fastest.
Arguments:
- hidden: bfloat16 [2, 1024, 8192], P('view', 'dp'), may hold values from -6 to 6
- weight: bfloat16 [8192, 8192], P(('view', 'dp'), 'unit'), may hold values from -4 to 4
Outputs:
- embedding: bfloat16 [2, 1024, 8192], P('view', 'dp', 'unit')
- weight_grad: float32 [8192, 8192], P(('view', 'dp'), 'unit')
- deviation: float32 [2, 8192], P('view', 'unit')
The draws below stay inside these ranges and needn't reach their ends.
All inputs are finite; a program needn't handle non-finite values.
Results may differ from the reference program's by a relative error of at most 0.025.
Values may be sent and summed in bfloat16 or wider, within the bound.
A program may use at most 64 MiB of HBM per device.

```python
import jax
import jax.numpy as jnp
from jax import lax

HID = 8192
EMB = 8192
IMG_DEV = 128
IMAGES = 1024
EMB_DEV = 512
N_DP = 8
N_UNIT = 16


def draw_weight(key, part):
    key = jax.random.fold_in(key, 7)
    first, second, third = jax.random.split(key, 3)
    base = jnp.clip(jax.random.normal(first, (HID, EMB), jnp.float32), -6.0, 6.0)
    upper = jax.random.bernoulli(second, 0.5, (EMB,))
    fraction = jax.random.uniform(third, (EMB,), jnp.float32)
    low_band = 0.25 * jnp.exp(fraction * jnp.log(2.8))
    high_band = 1.4 * jnp.exp(fraction * jnp.log(2.857))
    column_scale = jnp.where(upper, high_band, low_band)
    return (base * column_scale[None, :] / jnp.sqrt(jnp.float32(HID))).astype(jnp.bfloat16)


def shard_levels(own_key, dims, cuts, smallest, top_value):
    gain = 1.0
    for dim, parts in cuts:
        steps = jax.random.uniform(jax.random.fold_in(jax.random.fold_in(own_key, 6), dim), (parts,), jnp.float32, smallest / len(cuts), top_value / len(cuts))
        gain = gain * jnp.repeat(jnp.exp(steps), dims[dim] // parts).reshape((-1,) + (1,) * (len(dims) - 1 - dim))
    return gain


def gaussian(stream_key, extent, scale, limit, cuts=(), held_as=jnp.bfloat16):
    values = jax.random.normal(stream_key, extent, jnp.float32) * scale
    if len(cuts) > 0:
        values = shard_levels(stream_key, extent, cuts, -0.22, 0.18) * values
    return jnp.clip(values, min=-limit, max=limit).astype(held_as)


def setup_inputs(seed: int = 0) -> dict:
    keys = jax.random.split(jax.random.key(seed), 3)
    return {
        "hidden": gaussian(keys[0], (2, IMAGES, HID), 1.0, 6.0, ((0, 2), (1, 8))),
        "weight": draw_weight(jax.random.fold_in(keys[2], 71), 0),
    }


invariance_weight = 25.0
variance_weight = 25.0
covariance_weight = 1.0
variance_epsilon = 0.0001

def transposed_product(left, right):
    return lax.dot_general(left, right, (((0,), (0,)), ((), ())), preferred_element_type=jnp.float32)

def rounded_sum(total, part):
    part = lax.optimization_barrier(part.astype(jnp.bfloat16))
    return total + part.astype(jnp.float32)

def reference(hidden, weight):
    image_count = IMAGES
    loss_scale = IMAGES * EMB / 4096.0
    coefficient = 4.0 * covariance_weight * loss_scale / (EMB * (image_count - 1))
    embeds = [jnp.dot(hidden[view], weight, preferred_element_type=jnp.float32).astype(jnp.bfloat16) for view in range(2)]
    grads = []
    deviations = []
    for view in range(2):
        values = embeds[view].astype(jnp.float32)
        partner = embeds[1 - view].astype(jnp.float32)
        mean_values = lax.optimization_barrier(jnp.sum(values, 0)) / image_count
        centered = values - mean_values
        spread = lax.optimization_barrier(jnp.sum(centered * centered, 0)) / (image_count - 1)
        deviation = jnp.sqrt(spread + variance_epsilon)
        deviations.append(deviation)
        centered_half = centered.astype(jnp.bfloat16)
        shards = centered_half.reshape(N_DP, IMG_DEV, EMB)

        def block_grad(unit):
            start = unit * EMB_DEV
            columns = lax.dynamic_slice_in_dim(shards, start, EMB_DEV, 2)
            total = jnp.zeros((EMB, EMB_DEV), jnp.float32)
            for group in range(N_DP):
                total = rounded_sum(total, transposed_product(shards[group], columns[group]))
            tile = total / (image_count - 1)
            row_index = lax.broadcasted_iota(jnp.int32, tile.shape, 0)
            column_index = start + lax.broadcasted_iota(jnp.int32, tile.shape, 1)
            scaled = (jnp.where(row_index == column_index, 0.0, tile) * coefficient).astype(jnp.bfloat16)
            return jnp.dot(centered_half, scaled, preferred_element_type=jnp.float32)
        blocks = lax.map(block_grad, jnp.arange(N_UNIT, dtype=jnp.int32))
        covariance_grad = jnp.transpose(blocks, (1, 0, 2)).reshape(image_count, EMB)
        hinge = jnp.where(deviation < 1.0, centered / deviation, 0.0)
        direct = 2.0 * invariance_weight * (values - partner) / (image_count * EMB)
        spread_term = variance_weight / (2.0 * EMB * (image_count - 1)) * hinge
        grads.append((loss_scale * (direct - spread_term) + covariance_grad).astype(jnp.bfloat16))

    def weight_block(unit):
        start = unit * EMB_DEV
        total = jnp.zeros((HID, EMB_DEV), jnp.float32)
        for view in range(2):
            columns = lax.dynamic_slice_in_dim(grads[view], start, EMB_DEV, 1)
            for group in range(N_DP):
                feats = hidden[view, group * IMG_DEV:(group + 1) * IMG_DEV]
                slab = columns[group * IMG_DEV:(group + 1) * IMG_DEV]
                total = rounded_sum(total, transposed_product(feats, slab))
        return total
    wblocks = lax.map(weight_block, jnp.arange(N_UNIT, dtype=jnp.int32))
    weight_grad = jnp.transpose(wblocks, (1, 0, 2)).reshape(HID, EMB)
    return (jnp.stack(embeds), weight_grad, jnp.stack(deviations))
```

```python
import jax
import jax.numpy as jnp
from jax import lax
from jax.experimental import pallas as pl
from jax.experimental.pallas import tpu as pltpu
from jax.sharding import PartitionSpec as P

invariance_weight = 25.0
variance_weight = 25.0
covariance_weight = 1.0
variance_epsilon = 0.0001

IMG = 128
N = 8
SIDE = 4
WIDTH = 512
OUT = 8192
IMAGES = IMG * N
LOSS_SCALE = IMAGES * OUT / 4096.0
SLOT = {0: 0, 4: 1, 3: 2, 5: 3, 2: 4, 6: 5, 1: 6, 7: 7}
GROUPS = ((4,), (3, 5), (2, 6), (1, 7))
COPIES = 160


def transposed_product(left, right):
    return lax.dot_general(
        left, right, (((0,), (0,)), ((), ())), preferred_element_type=jnp.float32
    )


def product_transposed(left, right):
    return lax.dot_general(
        left, right, (((1,), (1,)), ((), ())), preferred_element_type=jnp.float32
    )


def kernel(
    hidden,
    weight,
    emb_out,
    mine_out,
    theirs_out,
    dev_out,
    feats,
    wgt,
    part,
    red_send,
    red_recv,
    emb,
    cen,
    partner,
    sums,
    gram,
    gram_half,
    gram_one,
    one_sum,
    gram_two,
    gram_all,
    grads,
    acc,
    give,
    local_sem,
    send_sem,
    recv_sem,
):
    v, j, u = lax.axis_index("view"), lax.axis_index("dp"), lax.axis_index("unit")
    x, y = u // SIDE, u % SIDE

    def at_z(k):
        return (v, (j + k + N) % N, u)

    def at_x(d):
        return (v, j, ((x + d) % SIDE) * SIDE + y)

    def at_y(d):
        return (v, j, x * SIDE + (y + d) % SIDE)

    other = (1 - v, j, u)
    copies = []

    def push(src, dst, device):
        i = len(copies)
        copy = pltpu.make_async_remote_copy(
            src_ref=src,
            dst_ref=dst,
            send_sem=send_sem.at[i],
            recv_sem=recv_sem.at[i],
            device_id=device,
            device_id_type=pl.DeviceIdType.MESH,
        )
        copy.start()
        copies.append(copy)
        return copy

    def m(value, by):
        return pl.multiple_of(value, by)

    loads = [
        pltpu.make_async_copy(
            hidden.at[0, :, pl.ds(m(c * (OUT // 2) + j * WIDTH, WIDTH), WIDTH)],
            feats.at[0, :, pl.ds(c * WIDTH, WIDTH)],
            local_sem.at[c],
        )
        for c in range(2)
    ]
    wrows = pl.ds(m(v * WIDTH, WIDTH), WIDTH)
    loads.append(pltpu.make_async_copy(weight, wgt.at[wrows], local_sem.at[2]))
    for load in loads:
        load.start()

    barrier = pltpu.get_barrier_semaphore()
    peers = [at_z(k) for k in range(1, N)]
    peers += [at_x(d) for d in range(1, SIDE)] + [at_y(d) for d in range(1, SIDE)] + [other]
    for peer in peers:
        pl.semaphore_signal(barrier, inc=1, device_id=peer, device_id_type=pl.DeviceIdType.MESH)
    pl.semaphore_wait(barrier, len(peers))

    a_rows, a_cols = pl.ds(m(16 * y, 16), 16), pl.ds(m(256 * x, 256), 256)
    b_rows, b_cols = pl.ds(m(64 + 16 * x, 16), 16), pl.ds(m(256 * y, 256), 256)
    first = {}
    for group in GROUPS:
        for k in group:
            to = (j - k + N) % N
            a_from = pl.ds(m((x // 2) * (OUT // 2) + to * WIDTH + (x % 2) * 256, 256), 256)
            b_from = pl.ds(m((y // 2) * (OUT // 2) + to * WIDTH + (y % 2) * 256, 256), 256)
            first[k] = (
                push(hidden.at[0, a_rows, a_from], feats.at[SLOT[k], a_rows, a_cols], at_z(-k)),
                push(hidden.at[0, b_rows, b_from], feats.at[SLOT[k], b_rows, b_cols], at_z(-k)),
            )
        if group == (4,):
            weight_copy = push(weight, wgt.at[wrows], other)

    def slots(group):
        return pl.ds(SLOT[group[0]], len(group))

    second, third, fourth = [], [], []
    for group in GROUPS:
        for k in group:
            for copy in first[k]:
                copy.wait_recv()
        a = feats.at[slots(group), a_rows, a_cols]
        b = feats.at[slots(group), b_rows, b_cols]
        second.append([c for d in (2, 1, 3) for c in (push(a, a, at_x(d)), push(b, b, at_y(d)))])
    for g, group in enumerate(GROUPS):
        for copy in second[g]:
            copy.wait_recv()
        a = feats.at[slots(group), a_rows, :]
        b = feats.at[slots(group), b_rows, :]
        third.append([c for d in (1, 3) for c in (push(a, a, at_y(d)), push(b, b, at_x(d)))])

    def pass_on(g):
        for copy in third[g]:
            copy.wait_recv()
        group = GROUPS[g]
        sent = []
        for d, c in ((1, 0), (3, WIDTH)):
            rows = pl.ds(m(16 * ((y - d + SIDE) % SIDE), 16), 16)
            a = feats.at[slots(group), rows, pl.ds(c, WIDTH)]
            sent.append(push(a, a, at_y(d)))
            rows = pl.ds(m(64 + 16 * ((x - d + SIDE) % SIDE), 16), 16)
            b = feats.at[slots(group), rows, pl.ds(c, WIDTH)]
            sent.append(push(b, b, at_x(d)))
        fourth.append(sent)

    def take(g):
        for copy in fourth[g]:
            copy.wait_recv()

    def project(k):
        part[SLOT[k]] = jnp.dot(
            feats[SLOT[k]], wgt[...], preferred_element_type=jnp.float32
        )

    low, high = pl.ds(0, 64), pl.ds(64, 64)

    def reduce_on(way, step, k, rows, before):
        half = 0 if rows is low else 1
        total = part[SLOT[k], rows, :]
        if before is not None:
            before.wait_recv()
            total = total + red_recv[way, step - 1, half].astype(jnp.float32)
        red_send[way, step, half] = total.astype(jnp.bfloat16)
        return push(
            red_send.at[way, step, half], red_recv.at[way, step, half], at_z(-1 if way == 0 else 1)
        )

    pass_on(0)
    for load in loads:
        load.wait()
    weight_copy.wait_recv()
    project(0)
    pass_on(1)
    take(0)
    project(4)
    down_low = reduce_on(0, 0, 4, low, None)
    up_high = reduce_on(1, 0, 4, high, None)
    pass_on(2)
    take(1)
    project(5)
    project(3)
    down_high = reduce_on(0, 1, 5, high, None)
    up_low = reduce_on(1, 1, 3, low, None)
    down_low = reduce_on(0, 1, 5, low, down_low)
    up_high = reduce_on(1, 1, 3, high, up_high)
    pass_on(3)
    for step, g, d, n in ((2, 2, 6, 2), (3, 3, 7, 1)):
        take(g)
        project(d)
        project(n)
        down_high = reduce_on(0, step, d, high, down_high)
        up_low = reduce_on(1, step, n, low, up_low)
        down_low = reduce_on(0, step, d, low, down_low)
        up_high = reduce_on(1, step, n, high, up_high)

    def finish(rows, half):
        total = part[0, rows, :] + (
            red_recv[0, 3, half].astype(jnp.float32) + red_recv[1, 3, half].astype(jnp.float32)
        )
        emb[rows, :] = total.astype(jnp.bfloat16)

    def start_gather(buf, rows):
        down = push(buf.at[rows], buf.at[pl.ds(IMG + rows.start, 64)], at_z(-1))
        up = push(buf.at[rows], buf.at[pl.ds(7 * IMG + rows.start, 64)], at_z(1))
        return down, up

    def rest_of_gather(buf, down, up, arrived):
        for step in range(1, 4):
            for h in (0, 1):
                down[h].wait_recv()
                if step < 3 or h == 0:
                    down[h] = push(
                        buf.at[pl.ds(step * IMG + 64 * h, 64)],
                        buf.at[pl.ds((step + 1) * IMG + 64 * h, 64)],
                        at_z(-1),
                    )
                up[1 - h].wait_recv()
                if step < 3 or h == 0:
                    up[1 - h] = push(
                        buf.at[pl.ds((N - step) * IMG + 64 * (1 - h), 64)],
                        buf.at[pl.ds((N - step - 1) * IMG + 64 * (1 - h), 64)],
                        at_z(1),
                    )
            arrived(step)
            arrived(N - step)
        down[0].wait_recv()
        up[1].wait_recv()
        arrived(4)

    down_high.wait_recv()
    up_high.wait_recv()
    finish(high, 1)
    down1, up1 = start_gather(emb, high)
    down_low.wait_recv()
    up_low.wait_recv()
    finish(low, 0)
    down0, up0 = start_gather(emb, low)
    partner_copy = push(emb.at[pl.ds(0, IMG)], partner, other)
    emb_out[0] = emb[pl.ds(0, IMG), :]

    def block(k):
        return pl.ds(k * IMG, IMG)

    def add_up(k):
        sums[pl.ds((j + k) % N, 1), :] = jnp.sum(
            emb[block(k), :].astype(jnp.float32), 0, keepdims=True
        )

    add_up(0)
    rest_of_gather(emb, [down0, down1], [up0, up1], add_up)
    mean_values = jnp.sum(sums[...], 0, keepdims=True) / IMAGES
    for k in range(N):
        centered = emb[block(k), :].astype(jnp.float32) - mean_values
        cen[block(k), :] = centered.astype(jnp.bfloat16)
        sums[pl.ds((j + k) % N, 1), :] = jnp.sum(centered * centered, 0, keepdims=True)
    deviation = jnp.sqrt(jnp.sum(sums[...], 0, keepdims=True) / (IMAGES - 1) + variance_epsilon)
    dev_out[...] = deviation

    for k in range(N):
        gram[:, block(k)] = product_transposed(cen[block(0), :], cen[block(k), :])
    gram_half[...] = gram[...].astype(jnp.bfloat16)
    one = []
    for d in (2, 1, 3):
        rows = pl.ds(m(16 * ((x + d) % SIDE), 16), 16)
        one.append(push(gram_half.at[rows], gram_one.at[0, d - 1], at_x(d)))
        rows = pl.ds(m(64 + 16 * ((y + d) % SIDE), 16), 16)
        one.append(push(gram_half.at[rows], gram_one.at[1, d - 1], at_y(d)))
    diagonal = jnp.zeros((1, WIDTH), jnp.float32)
    for k in range(N):
        half = cen[block(k), :].astype(jnp.float32)
        diagonal = diagonal + jnp.sum(half * half, 0, keepdims=True)
    for copy in one:
        copy.wait_recv()
    own = (pl.ds(m(16 * x, 16), 16), pl.ds(m(64 + 16 * y, 16), 16))
    for t in range(2):
        total = gram[own[t], :]
        for d in range(3):
            total = total + gram_one[t, d].astype(jnp.float32)
        one_sum[t] = total
        gram_half[own[t], :] = total.astype(jnp.bfloat16)
    two = []
    for d in (2, 1, 3):
        cols = pl.ds(m(256 * ((y + d) % SIDE), 256), 256)
        two.append(push(gram_half.at[own[0], cols], gram_two.at[0, d - 1], at_y(d)))
        cols = pl.ds(m(256 * ((x + d) % SIDE), 256), 256)
        two.append(push(gram_half.at[own[1], cols], gram_two.at[1, d - 1], at_x(d)))
    for copy in two:
        copy.wait_recv()
    piece = (pl.ds(m(256 * y, 256), 256), pl.ds(m(256 * x, 256), 256))
    for t in range(2):
        total = one_sum[t, :, piece[t]]
        for d in range(3):
            total = total + gram_two[t, d].astype(jnp.float32)
        gram_all[own[t], piece[t]] = total.astype(jnp.bfloat16)
    back = []
    for d in (2, 1, 3):
        ref = gram_all.at[own[0], piece[0]]
        back.append(push(ref, ref, at_y(d)))
        ref = gram_all.at[own[1], piece[1]]
        back.append(push(ref, ref, at_x(d)))
    for copy in back:
        copy.wait_recv()
    back = []
    for d in (2, 1, 3):
        ref = gram_all.at[own[0]]
        back.append(push(ref, ref, at_x(d)))
        ref = gram_all.at[own[1]]
        back.append(push(ref, ref, at_y(d)))
    for copy in back:
        copy.wait_recv()

    partner_copy.wait_recv()
    coefficient = 4.0 * covariance_weight * LOSS_SCALE / (OUT * (IMAGES - 1)) / (IMAGES - 1)
    hinge_scale = jnp.where(deviation < 1.0, 1.0 / deviation, 0.0) * (
        LOSS_SCALE * variance_weight / (2.0 * OUT * (IMAGES - 1))
    )
    direct_scale = LOSS_SCALE * 2.0 * invariance_weight / (IMAGES * OUT)

    def gradient(rows):
        covariance = jnp.dot(gram_all[rows, :], cen[...], preferred_element_type=jnp.float32)
        half = cen[rows, :].astype(jnp.float32)
        values = emb[rows, :].astype(jnp.float32)
        total = (
            direct_scale * (values - partner[rows, :].astype(jnp.float32))
            - hinge_scale * (values - mean_values)
            + coefficient * (covariance - half * diagonal)
        )
        grads[rows, :] = total.astype(jnp.bfloat16)

    gradient(high)
    down1, up1 = start_gather(grads, high)
    gradient(low)
    down0, up0 = start_gather(grads, low)
    acc[...] = transposed_product(feats[0], grads[block(0), :])

    def accumulate(k):
        acc[...] += transposed_product(feats[SLOT[k]], grads[block(k), :])

    rest_of_gather(grads, [down0, down1], [up0, up1], accumulate)

    give[...] = acc[pl.ds(m((1 - v) * WIDTH, WIDTH), WIDTH), :].astype(jnp.bfloat16)
    last = push(give, theirs_out, other)
    mine_out[...] = acc[wrows, :]
    last.wait_recv()
    for copy in copies:
        copy.wait_send()
    assert len(copies) <= COPIES


def per_device(hidden, weight):
    vmem = pl.BlockSpec(memory_space=pltpu.VMEM)
    hbm = pl.BlockSpec(memory_space=pl.ANY)
    half, full = jnp.bfloat16, jnp.float32
    emb, mine, theirs, dev = pl.pallas_call(
        kernel,
        out_shape=(
            jax.ShapeDtypeStruct((1, IMG, WIDTH), half),
            jax.ShapeDtypeStruct((WIDTH, WIDTH), full),
            jax.ShapeDtypeStruct((WIDTH, WIDTH), half),
            jax.ShapeDtypeStruct((1, WIDTH), full),
        ),
        in_specs=[hbm, hbm],
        out_specs=(vmem, vmem, vmem, vmem),
        scratch_shapes=[
            pltpu.VMEM((N, IMG, 2 * WIDTH), half),
            pltpu.VMEM((2 * WIDTH, WIDTH), half),
            pltpu.VMEM((N, IMG, WIDTH), full),
            pltpu.VMEM((2, 4, 2, 64, WIDTH), half),
            pltpu.VMEM((2, 4, 2, 64, WIDTH), half),
            pltpu.VMEM((IMAGES, WIDTH), half),
            pltpu.VMEM((IMAGES, WIDTH), half),
            pltpu.VMEM((IMG, WIDTH), half),
            pltpu.VMEM((N, WIDTH), full),
            pltpu.VMEM((IMG, IMAGES), full),
            pltpu.VMEM((IMG, IMAGES), half),
            pltpu.VMEM((2, 3, 16, IMAGES), half),
            pltpu.VMEM((2, 16, IMAGES), full),
            pltpu.VMEM((2, 3, 16, 256), half),
            pltpu.VMEM((IMG, IMAGES), half),
            pltpu.VMEM((IMAGES, WIDTH), half),
            pltpu.VMEM((2 * WIDTH, WIDTH), full),
            pltpu.VMEM((WIDTH, WIDTH), half),
            pltpu.SemaphoreType.DMA((3,)),
            pltpu.SemaphoreType.DMA((COPIES,)),
            pltpu.SemaphoreType.DMA((COPIES,)),
        ],
        compiler_params=pltpu.CompilerParams(
            collective_id=0, has_side_effects=True, vmem_limit_bytes=48 << 20
        ),
        name="expander",
    )(hidden, weight)
    return emb, mine + theirs.astype(jnp.float32), dev


def solution(mesh):
    placed = (P("view", "dp", None), P(("view", "dp"), "unit"))
    return jax.shard_map(
        per_device,
        mesh=mesh,
        in_specs=placed,
        out_specs=(P("view", "dp", "unit"), P(("view", "dp"), "unit"), P("view", "unit")),
        check_vma=False,
    )
```

```python
import jax
import jax.numpy as jnp
from jax import lax
from jax.experimental import pallas as pl
from jax.experimental.pallas import tpu as pltpu
from jax.sharding import PartitionSpec as P

invariance_weight = 25.0
variance_weight = 25.0
covariance_weight = 1.0
variance_epsilon = 0.0001

IMG = 128
N = 8
SIDE = 4
WIDTH = 512
OUT = 8192
IMAGES = IMG * N
LOSS_SCALE = IMAGES * OUT / 4096.0
SLOT = {0: 0, 4: 1, 3: 2, 5: 3, 2: 4, 6: 5, 1: 6, 7: 7}
PLACE = {0: 0, 1: 1, 7: 2, 2: 3, 6: 4, 3: 5, 5: 6, 4: 7}
GROUPS = ((4,), (3, 5), (2, 6), (1, 7))
EARLY, LATE = 5 * IMG, 7 * IMG
WAITS = 72
SENDS = 16


def transposed_product(left, right):
    return lax.dot_general(
        left, right, (((0,), (0,)), ((), ())), preferred_element_type=jnp.float32
    )


def product_transposed(left, right):
    return lax.dot_general(
        left, right, (((1,), (1,)), ((), ())), preferred_element_type=jnp.float32
    )


def kernel(
    hidden,
    weight,
    emb_out,
    grad_out,
    dev_out,
    feats,
    wgt,
    part,
    red_send,
    red_recv,
    emb,
    cen,
    partner,
    sums,
    squares,
    gram,
    gram_half,
    gram_one,
    gram_sum,
    gram_two,
    last_part,
    last_sum,
    gram_all,
    grads,
    acc,
    mine,
    give,
    theirs,
    local_sem,
    send_sem,
    recv_sem,
):
    v, j, u = lax.axis_index("view"), lax.axis_index("dp"), lax.axis_index("unit")
    x, y = u // SIDE, u % SIDE

    def at_z(k):
        return (v, (j + k + N) % N, u)

    def at_x(d):
        return (v, j, ((x + d) % SIDE) * SIDE + y)

    def at_y(d):
        return (v, j, x * SIDE + (y + d) % SIDE)

    other = (1 - v, j, u)
    groups, sends = [], {}

    class Group:
        def __init__(self, name, like):
            self.at, self.name, self.like = len(groups), name, like
            groups.append(self)
            sends.setdefault(name, len(sends))

        def push(self, src, dst, device):
            pltpu.make_async_remote_copy(
                src_ref=src,
                dst_ref=dst,
                send_sem=send_sem.at[sends[self.name]],
                recv_sem=recv_sem.at[self.at],
                device_id=device,
                device_id_type=pl.DeviceIdType.MESH,
            ).start()

        def wait_recv(self):
            pltpu.make_async_copy(self.like, self.like, recv_sem.at[self.at]).wait()

    def push(name, src, dst, device):
        group = Group(name, src)
        group.push(src, dst, device)
        return group

    def wait_sends(name, like):
        pltpu.make_async_copy(like, like, send_sem.at[sends.pop(name)]).wait()

    def m(value, by):
        return pl.multiple_of(value, by)

    def slots(group):
        return pl.ds(SLOT[group[0]], len(group))

    loads = [
        pltpu.make_async_copy(
            hidden.at[0, :, pl.ds(m(c * (OUT // 2) + j * WIDTH, WIDTH), WIDTH)],
            feats.at[0, :, pl.ds(c * WIDTH, WIDTH)],
            local_sem.at[c],
        )
        for c in range(2)
    ]
    wrows = pl.ds(m(v * WIDTH, WIDTH), WIDTH)
    orows = pl.ds(m((1 - v) * WIDTH, WIDTH), WIDTH)
    loads.append(pltpu.make_async_copy(weight, wgt.at[wrows], local_sem.at[2]))
    for load in loads:
        load.start()

    barrier = pltpu.get_barrier_semaphore()
    peers = [at_z(k) for k in range(1, N)]
    peers += [at_x(d) for d in range(1, SIDE)] + [at_y(d) for d in range(1, SIDE)] + [other]
    for peer in peers:
        pl.semaphore_signal(barrier, inc=1, device_id=peer, device_id_type=pl.DeviceIdType.MESH)
    pl.semaphore_wait(barrier, len(peers))

    a_rows, a_cols = pl.ds(m(16 * y, 16), 16), pl.ds(m(256 * x, 256), 256)
    b_rows, b_cols = pl.ds(m(64 + 16 * x, 16), 16), pl.ds(m(256 * y, 256), 256)
    first = []
    for group in GROUPS:
        first.append(Group("first", feats.at[slots(group), pl.ds(0, 32), pl.ds(0, 256)]))
        for k in group:
            to = (j - k + N) % N
            a_from = pl.ds(m((x // 2) * (OUT // 2) + to * WIDTH + (x % 2) * 256, 256), 256)
            b_from = pl.ds(m((y // 2) * (OUT // 2) + to * WIDTH + (y % 2) * 256, 256), 256)
            a_to, b_to = feats.at[SLOT[k], a_rows, a_cols], feats.at[SLOT[k], b_rows, b_cols]
            first[-1].push(hidden.at[0, a_rows, a_from], a_to, at_z(-k))
            first[-1].push(hidden.at[0, b_rows, b_from], b_to, at_z(-k))
        if group == (4,):
            weight_copy = push("weight", weight, wgt.at[wrows], other)

    def project(k):
        part[SLOT[k]] = jnp.dot(feats[SLOT[k]], wgt[...], preferred_element_type=jnp.float32)

    for load in loads:
        load.wait()
    weight_copy.wait_recv()
    project(0)

    second, third = [], []

    def along_one(g):
        group = GROUPS[g]
        first[g].wait_recv()
        a = feats.at[slots(group), a_rows, a_cols]
        b = feats.at[slots(group), b_rows, b_cols]
        second.append(Group("second", feats.at[slots(group), pl.ds(0, 96), pl.ds(0, 256)]))
        for d in (2, 1, 3):
            second[g].push(a, a, at_x(d))
            second[g].push(b, b, at_y(d))

    def along_both(g):
        group = GROUPS[g]
        second[g].wait_recv()
        a = feats.at[slots(group), a_rows, :]
        b = feats.at[slots(group), b_rows, :]
        third.append(Group("third", feats.at[slots(group), pl.ds(0, 96), :]))
        for d in (2, 1, 3):
            third[g].push(a, a, at_y(d))
            third[g].push(b, b, at_x(d))

    def take(g):
        third[g].wait_recv()

    low, high = pl.ds(0, 64), pl.ds(64, 64)

    def reduce_on(way, step, k, rows, before):
        half = 0 if rows is low else 1
        total = part[SLOT[k], rows, :]
        if before is not None:
            before.wait_recv()
            total = total + red_recv[way, step - 1, half].astype(jnp.float32)
        red_send[way, step, half] = total.astype(jnp.bfloat16)
        return push(
            "reduce", red_send.at[way, step, half], red_recv.at[way, step, half], at_z(-1 if way == 0 else 1)
        )

    along_one(0)
    along_one(1)
    along_one(2)
    along_both(0)
    along_both(1)
    along_one(3)
    take(0)
    project(4)
    down_low = reduce_on(0, 0, 4, low, None)
    up_high = reduce_on(1, 0, 4, high, None)
    along_both(2)
    take(1)
    project(5)
    down_high = reduce_on(0, 1, 5, high, None)
    project(3)
    up_low = reduce_on(1, 1, 3, low, None)
    down_low = reduce_on(0, 1, 5, low, down_low)
    up_high = reduce_on(1, 1, 3, high, up_high)
    along_both(3)
    for step, g, d, n in ((2, 2, 6, 2), (3, 3, 7, 1)):
        take(g)
        project(d)
        project(n)
        down_high = reduce_on(0, step, d, high, down_high)
        up_low = reduce_on(1, step, n, low, up_low)
        down_low = reduce_on(0, step, d, low, down_low)
        up_high = reduce_on(1, step, n, high, up_high)

    def finish(rows, half):
        total = part[0, rows, :] + (
            red_recv[0, 3, half].astype(jnp.float32) + red_recv[1, 3, half].astype(jnp.float32)
        )
        emb[rows, :] = total.astype(jnp.bfloat16)

    def block(k):
        return pl.ds(PLACE[k] * IMG, IMG)

    def half_block(k, h):
        return pl.ds(PLACE[k] * IMG + 64 * h, 64)

    def start_gather(name, buf):
        down, up = [None, None], [None, None]
        for h in (0, 1):
            down[h] = push(name, buf.at[half_block(0, h)], buf.at[half_block(1, h)], at_z(-1))
            up[1 - h] = push(
                name, buf.at[half_block(0, 1 - h)], buf.at[half_block(7, 1 - h)], at_z(1)
            )
        return down, up

    def gather_step(name, buf, step, down, up, between=None):
        for h in (0, 1):
            down[h].wait_recv()
            if step < 3 or h == 0:
                down[h] = push(
                    name, buf.at[half_block(step, h)], buf.at[half_block(step + 1, h)], at_z(-1)
                )
            up[1 - h].wait_recv()
            if step < 3 or h == 0:
                up[1 - h] = push(
                    name,
                    buf.at[half_block(N - step, 1 - h)],
                    buf.at[half_block(N - step - 1, 1 - h)],
                    at_z(1),
                )
            if h == 0 and between is not None:
                between()

    down_high.wait_recv()
    up_low.wait_recv()
    down_low.wait_recv()
    finish(low, 0)
    up_high.wait_recv()
    finish(high, 1)
    down, up = start_gather("emb", emb)
    sums[pl.ds(j, 1)] = jnp.sum(emb[block(0), :].astype(jnp.float32), 0, keepdims=True)[None]
    shares = Group("shares", sums.at[pl.ds(0, N - 1)])
    for k in (4, 3, 5, 2, 6, 1, 7):
        shares.push(sums.at[pl.ds(j, 1)], sums.at[pl.ds(j, 1)], at_z(k))
    partner_copy = push("partner", emb.at[block(0)], partner, other)
    emb_out[0] = emb[block(0), :]

    gather_step("emb", emb, 1, down, up)
    gather_step("emb", emb, 2, down, up)
    shares.wait_recv()
    mean_values = jnp.sum(sums[...], 0) / IMAGES

    def center(k):
        centered = emb[block(k), :].astype(jnp.float32) - mean_values
        half = centered.astype(jnp.bfloat16)
        cen[block(k), :] = half
        half = half.astype(jnp.float32)
        squares[0, pl.ds((j + k) % N, 1), :] = jnp.sum(centered * centered, 0, keepdims=True)
        squares[1, pl.ds((j + k) % N, 1), :] = jnp.sum(half * half, 0, keepdims=True)

    def multiply(k):
        product = product_transposed(cen[block(0), :], cen[block(k), :])
        gram[:, block(k)] = product
        gram_half[:, block(k)] = product.astype(jnp.bfloat16)

    own = (pl.ds(m(16 * x, 16), 16), pl.ds(m(64 + 16 * y, 16), 16))
    early, middle, late = pl.ds(0, EARLY), pl.ds(EARLY, LATE - EARLY), pl.ds(LATE, IMG)

    def scatter(cols):
        group = Group("scatter", gram_half.at[pl.ds(0, 96), cols])
        for d in (2, 1, 3):
            rows = pl.ds(m(16 * ((x + d) % SIDE), 16), 16)
            group.push(gram_half.at[rows, cols], gram_one.at[0, d - 1, :, cols], at_x(d))
            rows = pl.ds(m(64 + 16 * ((y + d) % SIDE), 16), 16)
            group.push(gram_half.at[rows, cols], gram_one.at[1, d - 1, :, cols], at_y(d))
        return group

    def spread(cols, before):
        before.wait_recv()
        group = Group("spread", gram_half.at[pl.ds(0, 96), cols])
        for t in range(2):
            total = gram[own[t], cols]
            for d in range(3):
                total = total + gram_one[t, d, :, cols].astype(jnp.float32)
            gram_sum[t, :, cols] = total.astype(jnp.bfloat16)
        for d in (2, 1, 3):
            group.push(gram_sum.at[0, :, cols], gram_two.at[0, d - 1, :, cols], at_y(d))
            group.push(gram_sum.at[1, :, cols], gram_two.at[1, d - 1, :, cols], at_x(d))
        return group

    def collect(cols, before):
        before.wait_recv()
        group = Group("collect", gram_half.at[pl.ds(0, 96), cols])
        for t in range(2):
            total = gram_sum[t, :, cols].astype(jnp.float32)
            for d in range(3):
                total = total + gram_two[t, d, :, cols].astype(jnp.float32)
            gram_all[own[t], cols] = total.astype(jnp.bfloat16)
        for d in (2, 1, 3):
            ref = gram_all.at[own[0], cols]
            group.push(ref, ref, at_x(d))
            ref = gram_all.at[own[1], cols]
            group.push(ref, ref, at_y(d))
        return group

    def last_one():
        group = Group("last_one", gram_half.at[:, pl.ds(0, 3 * IMG)])
        for d in (2, 1, 3):
            group.push(gram_half.at[low, late], last_part.at[0, d - 1], at_x(d))
            group.push(gram_half.at[high, late], last_part.at[1, d - 1], at_y(d))
        return group

    def last_two(before):
        before.wait_recv()
        group = Group("last_two", gram_half.at[:, pl.ds(0, 3 * IMG)])
        for t, rows in enumerate((low, high)):
            total = gram_half[rows, late].astype(jnp.float32)
            for d in range(3):
                total = total + last_part[t, d].astype(jnp.float32)
            last_sum[t] = total.astype(jnp.bfloat16)
        for d in (2, 1, 3):
            group.push(last_sum.at[0], last_part.at[2, d - 1], at_y(d))
            group.push(last_sum.at[1], last_part.at[3, d - 1], at_x(d))
        return group

    def last_end(before):
        before.wait_recv()
        for t, rows in enumerate((low, high)):
            total = last_sum[t].astype(jnp.float32)
            for d in range(3):
                total = total + last_part[2 + t, d].astype(jnp.float32)
            gram_all[rows, late] = total.astype(jnp.bfloat16)

    for k in (0, 1, 7):
        center(k)
    parts = []

    def in_third():
        for k in (0, 1, 7):
            multiply(k)
        for k in (2, 6):
            center(k)
            multiply(k)
        parts.append(scatter(early))

    gather_step("emb", emb, 3, down, up, in_third)
    for k in (3, 5):
        center(k)
        multiply(k)
    parts.append(scatter(middle))
    parts[0] = spread(early, parts[0])
    down[0].wait_recv()
    up[1].wait_recv()
    center(4)
    multiply(4)
    final = last_one()
    parts[1] = spread(middle, parts[1])
    deviation = jnp.sqrt(
        jnp.sum(squares[0], 0, keepdims=True) / (IMAGES - 1) + variance_epsilon
    )
    dev_out[...] = deviation
    diagonal = jnp.sum(squares[1], 0, keepdims=True)
    parts[0] = collect(early, parts[0])
    final = last_two(final)
    parts[1] = collect(middle, parts[1])
    partner_copy.wait_recv()
    parts[0].wait_recv()
    before_last = pl.ds(0, EARLY)
    covariance_part = jnp.dot(
        gram_all[:, before_last], cen[before_last, :], preferred_element_type=jnp.float32
    )
    part[0] = covariance_part
    last_end(final)
    parts[1].wait_recv()

    coefficient = 4.0 * covariance_weight * LOSS_SCALE / (OUT * (IMAGES - 1)) / (IMAGES - 1)
    hinge_scale = jnp.where(deviation < 1.0, 1.0 / deviation, 0.0) * (
        LOSS_SCALE * variance_weight / (2.0 * OUT * (IMAGES - 1))
    )
    direct_scale = LOSS_SCALE * 2.0 * invariance_weight / (IMAGES * OUT)

    def gradient(rows):
        rest = pl.ds(EARLY, IMAGES - EARLY)
        covariance = part[0, rows, :] + jnp.dot(
            gram_all[rows, rest], cen[rest, :], preferred_element_type=jnp.float32
        )
        half = cen[rows, :].astype(jnp.float32)
        values = emb[rows, :].astype(jnp.float32)
        total = (
            direct_scale * (values - partner[rows, :].astype(jnp.float32))
            - hinge_scale * (values - mean_values)
            + coefficient * (covariance - half * diagonal)
        )
        grads[rows, :] = total.astype(jnp.bfloat16)

    gradient(low)
    gradient(high)
    down, up = start_gather("grads", grads)

    def times(ks, cols):
        n = len(ks)
        left = feats[pl.ds(SLOT[ks[0]], n), :, cols].reshape(n * IMG, WIDTH)
        right = grads[pl.ds(PLACE[ks[0]] * IMG, n * IMG), :]
        return transposed_product(left, right)

    acc[...] = times((0,), orows)
    mine[...] = times((0,), wrows)
    for step in range(1, 4):
        gather_step("grads", grads, step, down, up)
        acc[...] += times((step, N - step), orows)
        mine[...] += times((step, N - step), wrows)
    down[0].wait_recv()
    up[1].wait_recv()

    give[...] = (acc[...] + times((4,), orows)).astype(jnp.bfloat16)
    last = push("last", give, theirs, other)
    mine[...] += times((4,), wrows)
    seven = pl.ds(1, N - 1)
    wait_sends("first", feats.at[seven, pl.ds(0, 32), pl.ds(0, 256)])
    wait_sends("second", feats.at[seven, pl.ds(0, 96), pl.ds(0, 256)])
    wait_sends("third", feats.at[seven, pl.ds(0, 96), :])
    wait_sends("weight", weight)
    wait_sends("reduce", emb.at[pl.ds(0, 7 * IMG)])
    wait_sends("emb", emb.at[pl.ds(0, 7 * IMG)])
    wait_sends("grads", emb.at[pl.ds(0, 7 * IMG)])
    wait_sends("shares", sums.at[pl.ds(0, N - 1)])
    wait_sends("partner", partner)
    for name in ("scatter", "spread", "collect"):
        wait_sends(name, gram_half.at[pl.ds(0, 96), pl.ds(0, LATE)])
    for name in ("last_one", "last_two"):
        wait_sends(name, gram_half.at[:, pl.ds(0, 3 * IMG)])
    last.wait_recv()
    grad_out[...] = mine[...] + theirs[...].astype(jnp.float32)
    wait_sends("last", give)
    assert not sends and len(groups) <= WAITS


def per_device(hidden, weight):
    vmem = pl.BlockSpec(memory_space=pltpu.VMEM)
    hbm = pl.BlockSpec(memory_space=pltpu.HBM)
    half, full = jnp.bfloat16, jnp.float32
    return pl.pallas_call(
        kernel,
        out_shape=(
            jax.ShapeDtypeStruct((1, IMG, WIDTH), half),
            jax.ShapeDtypeStruct((WIDTH, WIDTH), full),
            jax.ShapeDtypeStruct((1, WIDTH), full),
        ),
        in_specs=[hbm, hbm],
        out_specs=(vmem, vmem, vmem),
        scratch_shapes=[
            pltpu.VMEM((N, IMG, 2 * WIDTH), half),
            pltpu.VMEM((2 * WIDTH, WIDTH), half),
            pltpu.VMEM((N, IMG, WIDTH), full),
            pltpu.VMEM((2, 4, 2, 64, WIDTH), half),
            pltpu.VMEM((2, 4, 2, 64, WIDTH), half),
            pltpu.VMEM((IMAGES, WIDTH), half),
            pltpu.VMEM((IMAGES, WIDTH), half),
            pltpu.VMEM((IMG, WIDTH), half),
            pltpu.VMEM((N, 1, WIDTH), full),
            pltpu.VMEM((2, N, WIDTH), full),
            pltpu.VMEM((IMG, IMAGES), full),
            pltpu.VMEM((IMG, IMAGES), half),
            pltpu.VMEM((2, 3, 16, IMAGES), half),
            pltpu.VMEM((2, 16, IMAGES), half),
            pltpu.VMEM((2, 3, 16, IMAGES), half),
            pltpu.VMEM((4, 3, 64, IMG), half),
            pltpu.VMEM((2, 64, IMG), half),
            pltpu.VMEM((IMG, IMAGES), half),
            pltpu.VMEM((IMAGES, WIDTH), half),
            pltpu.VMEM((WIDTH, WIDTH), full),
            pltpu.VMEM((WIDTH, WIDTH), full),
            pltpu.VMEM((WIDTH, WIDTH), half),
            pltpu.VMEM((WIDTH, WIDTH), half),
            pltpu.SemaphoreType.DMA((3,)),
            pltpu.SemaphoreType.DMA((SENDS,)),
            pltpu.SemaphoreType.DMA((WAITS,)),
        ],
        compiler_params=pltpu.CompilerParams(
            collective_id=0, has_side_effects=True, vmem_limit_bytes=48 << 20
        ),
        name="expander",
    )(hidden, weight)


def solution(mesh):
    placed = (P("view", "dp", None), P(("view", "dp"), "unit"))
    return jax.shard_map(
        per_device,
        mesh=mesh,
        in_specs=placed,
        out_specs=(P("view", "dp", "unit"), P(("view", "dp"), "unit"), P("view", "unit")),
        check_vma=False,
    )
```

```python
import jax
import jax.numpy as jnp
from jax import lax
from jax.experimental import pallas as pl
from jax.experimental.pallas import tpu as pltpu
from jax.sharding import PartitionSpec as P

invariance_weight = 25.0
variance_weight = 25.0
covariance_weight = 1.0
variance_epsilon = 0.0001

IMG = 128
N = 8
SIDE = 4
WIDTH = 512
OUT = 8192
IMAGES = IMG * N
LOSS_SCALE = IMAGES * OUT / 4096.0
SLOT = {0: 0, 4: 1, 3: 2, 5: 3, 2: 4, 6: 5, 1: 6, 7: 7}
PLACE = {0: 0, 1: 1, 7: 2, 2: 3, 6: 4, 3: 5, 5: 6, 4: 7}
GROUPS = ((4,), (3, 5), (2, 6))
EARLY, LATE = 5 * IMG, 7 * IMG
WAITS = 72
SENDS = 16


def transposed_product(left, right):
    return lax.dot_general(
        left, right, (((0,), (0,)), ((), ())), preferred_element_type=jnp.float32
    )


def product_transposed(left, right):
    return lax.dot_general(
        left, right, (((1,), (1,)), ((), ())), preferred_element_type=jnp.float32
    )


def kernel(
    hidden,
    weight,
    emb_out,
    grad_out,
    dev_out,
    held,
    feats,
    wgt,
    part,
    red_send,
    red_recv,
    emb,
    cen,
    partner,
    sums,
    squares,
    gram,
    gram_half,
    gram_one,
    gram_sum,
    gram_two,
    last_part,
    last_sum,
    gram_all,
    grads,
    acc,
    mine,
    give,
    theirs,
    local_sem,
    send_sem,
    recv_sem,
):
    v, j, u = lax.axis_index("view"), lax.axis_index("dp"), lax.axis_index("unit")
    x, y = u // SIDE, u % SIDE

    def at_z(k):
        return (v, (j + k + N) % N, u)

    def at_x(d):
        return (v, j, ((x + d) % SIDE) * SIDE + y)

    def at_y(d):
        return (v, j, x * SIDE + (y + d) % SIDE)

    other = (1 - v, j, u)
    groups, sends = [], {}

    class Group:
        def __init__(self, name, like):
            self.at, self.name, self.like = len(groups), name, like
            groups.append(self)
            sends.setdefault(name, len(sends))

        def push(self, src, dst, device):
            pltpu.make_async_remote_copy(
                src_ref=src,
                dst_ref=dst,
                send_sem=send_sem.at[sends[self.name]],
                recv_sem=recv_sem.at[self.at],
                device_id=device,
                device_id_type=pl.DeviceIdType.MESH,
            ).start()

        def wait_recv(self):
            pltpu.make_async_copy(self.like, self.like, recv_sem.at[self.at]).wait()

    def push(name, src, dst, device):
        group = Group(name, src)
        group.push(src, dst, device)
        return group

    def wait_sends(name, like):
        pltpu.make_async_copy(like, like, send_sem.at[sends.pop(name)]).wait()

    def m(value, by):
        return pl.multiple_of(value, by)

    def slots(group):
        return pl.ds(SLOT[group[0]], len(group))

    wrows = pl.ds(m(v * WIDTH, WIDTH), WIDTH)
    orows = pl.ds(m((1 - v) * WIDTH, WIDTH), WIDTH)
    load_hidden = pltpu.make_async_copy(hidden.at[0], held, local_sem.at[0])
    load_weight = pltpu.make_async_copy(weight, wgt.at[wrows], local_sem.at[1])
    load_hidden.start()
    load_weight.start()

    def columns_of(block, c):
        return pl.ds(m(c * (OUT // 2) + block * WIDTH, WIDTH), WIDTH)

    barrier = pltpu.get_barrier_semaphore()
    peers = [at_z(k) for k in range(1, N)]
    peers += [at_x(d) for d in range(1, SIDE)] + [at_y(d) for d in range(1, SIDE)] + [other]
    for peer in peers:
        pl.semaphore_signal(barrier, inc=1, device_id=peer, device_id_type=pl.DeviceIdType.MESH)
    pl.semaphore_wait(barrier, len(peers))

    a_rows, a_cols = pl.ds(m(16 * y, 16), 16), pl.ds(m(256 * x, 256), 256)
    b_rows, b_cols = pl.ds(m(64 + 16 * x, 16), 16), pl.ds(m(256 * y, 256), 256)
    load_hidden.wait()
    first = []
    for group in GROUPS:
        first.append(Group("first", feats.at[slots(group), pl.ds(0, 32), pl.ds(0, 256)]))
        for k in group:
            to = (j - k + N) % N
            a_from = pl.ds(m((x // 2) * (OUT // 2) + to * WIDTH + (x % 2) * 256, 256), 256)
            b_from = pl.ds(m((y // 2) * (OUT // 2) + to * WIDTH + (y % 2) * 256, 256), 256)
            a_to, b_to = feats.at[SLOT[k], a_rows, a_cols], feats.at[SLOT[k], b_rows, b_cols]
            first[-1].push(held.at[a_rows, a_from], a_to, at_z(-k))
            first[-1].push(held.at[b_rows, b_from], b_to, at_z(-k))
        if group == (4,):
            load_weight.wait()
            weight_copy = push("weight", wgt.at[wrows], wgt.at[wrows], other)

    def project(k):
        part[SLOT[k]] = jnp.dot(feats[SLOT[k]], wgt[...], preferred_element_type=jnp.float32)

    for c in range(2):
        feats[0, :, pl.ds(c * WIDTH, WIDTH)] = held[:, columns_of(j, c)]
    weight_copy.wait_recv()
    project(0)

    second, third = [], []

    def along_one(g):
        group = GROUPS[g]
        first[g].wait_recv()
        a = feats.at[slots(group), a_rows, a_cols]
        b = feats.at[slots(group), b_rows, b_cols]
        second.append(Group("second", feats.at[slots(group), pl.ds(0, 96), pl.ds(0, 256)]))
        for d in (2, 1, 3):
            second[g].push(a, a, at_x(d))
            second[g].push(b, b, at_y(d))

    def along_both(g):
        group = GROUPS[g]
        second[g].wait_recv()
        a = feats.at[slots(group), a_rows, :]
        b = feats.at[slots(group), b_rows, :]
        third.append(Group("third", feats.at[slots(group), pl.ds(0, 96), :]))
        for d in (2, 1, 3):
            third[g].push(a, a, at_y(d))
            third[g].push(b, b, at_x(d))

    def take(g):
        third[g].wait_recv()

    low, high = pl.ds(0, 64), pl.ds(64, 64)

    def reduce_on(way, step, k, rows, before):
        half = 0 if rows is low else 1
        total = part[SLOT[k], rows, :]
        if before is not None:
            before.wait_recv()
            total = total + red_recv[way, step - 1, half].astype(jnp.float32)
        red_send[way, step, half] = total.astype(jnp.bfloat16)
        return push(
            "reduce", red_send.at[way, step, half], red_recv.at[way, step, half], at_z(-1 if way == 0 else 1)
        )

    along_one(0)
    along_one(1)
    near = Group("near", feats.at[slots((1, 7))])
    for c in range(2):
        for k in (1, 7):
            to = (j - k + N) % N
            at = feats.at[SLOT[k], :, pl.ds(c * WIDTH, WIDTH)]
            near.push(held.at[:, columns_of(to, c)], at, at_z(-k))
    along_one(2)
    along_both(0)
    along_both(1)
    take(0)
    project(4)
    down_low = reduce_on(0, 0, 4, low, None)
    up_high = reduce_on(1, 0, 4, high, None)
    along_both(2)
    take(1)
    project(5)
    down_high = reduce_on(0, 1, 5, high, None)
    project(3)
    up_low = reduce_on(1, 1, 3, low, None)
    down_low = reduce_on(0, 1, 5, low, down_low)
    up_high = reduce_on(1, 1, 3, high, up_high)
    for step, d, n in ((2, 6, 2), (3, 7, 1)):
        if step == 2:
            take(2)
        else:
            near.wait_recv()
        project(d)
        project(n)
        down_high = reduce_on(0, step, d, high, down_high)
        up_low = reduce_on(1, step, n, low, up_low)
        down_low = reduce_on(0, step, d, low, down_low)
        up_high = reduce_on(1, step, n, high, up_high)

    def finish(rows, half):
        total = part[0, rows, :] + (
            red_recv[0, 3, half].astype(jnp.float32) + red_recv[1, 3, half].astype(jnp.float32)
        )
        emb[rows, :] = total.astype(jnp.bfloat16)

    def block(k):
        return pl.ds(PLACE[k] * IMG, IMG)

    def half_block(k, h):
        return pl.ds(PLACE[k] * IMG + 64 * h, 64)

    def start_gather(name, buf, make):
        down, up = [None, None], [None, None]
        make(low, 0)
        down[0] = push(name, buf.at[half_block(0, 0)], buf.at[half_block(1, 0)], at_z(-1))
        make(high, 1)
        up[1] = push(name, buf.at[half_block(0, 1)], buf.at[half_block(7, 1)], at_z(1))
        down[1] = push(name, buf.at[half_block(0, 1)], buf.at[half_block(1, 1)], at_z(-1))
        up[0] = push(name, buf.at[half_block(0, 0)], buf.at[half_block(7, 0)], at_z(1))
        return down, up

    def gather_step(name, buf, step, down, up, between=None):
        for h in (0, 1):
            down[h].wait_recv()
            if step < 3 or h == 0:
                down[h] = push(
                    name, buf.at[half_block(step, h)], buf.at[half_block(step + 1, h)], at_z(-1)
                )
            up[1 - h].wait_recv()
            if step < 3 or h == 0:
                up[1 - h] = push(
                    name,
                    buf.at[half_block(N - step, 1 - h)],
                    buf.at[half_block(N - step - 1, 1 - h)],
                    at_z(1),
                )
            if h == 0 and between is not None:
                between()

    down_high.wait_recv()
    up_low.wait_recv()

    def reduced(rows, half):
        (down_low if half == 0 else up_high).wait_recv()
        finish(rows, half)

    down, up = start_gather("emb", emb, reduced)
    sums[pl.ds(j, 1)] = jnp.sum(emb[block(0), :].astype(jnp.float32), 0, keepdims=True)[None]
    shares = Group("shares", sums.at[pl.ds(0, N - 1)])
    for k in (4, 3, 5, 2, 6, 1, 7):
        shares.push(sums.at[pl.ds(j, 1)], sums.at[pl.ds(j, 1)], at_z(k))
    partner_copy = push("partner", emb.at[block(0)], partner, other)
    emb_out[0] = emb[block(0), :]

    gather_step("emb", emb, 1, down, up)
    gather_step("emb", emb, 2, down, up)
    shares.wait_recv()
    mean_values = jnp.sum(sums[...], 0) / IMAGES

    def center(k):
        centered = emb[block(k), :].astype(jnp.float32) - mean_values
        half = centered.astype(jnp.bfloat16)
        cen[block(k), :] = half
        half = half.astype(jnp.float32)
        squares[0, pl.ds((j + k) % N, 1), :] = jnp.sum(centered * centered, 0, keepdims=True)
        squares[1, pl.ds((j + k) % N, 1), :] = jnp.sum(half * half, 0, keepdims=True)

    def multiply(k):
        product = product_transposed(cen[block(0), :], cen[block(k), :])
        gram[:, block(k)] = product
        gram_half[:, block(k)] = product.astype(jnp.bfloat16)

    own = (pl.ds(m(16 * x, 16), 16), pl.ds(m(64 + 16 * y, 16), 16))
    early, middle, late = pl.ds(0, EARLY), pl.ds(EARLY, LATE - EARLY), pl.ds(LATE, IMG)

    def scatter(cols):
        group = Group("scatter", gram_half.at[pl.ds(0, 96), cols])
        for d in (2, 1, 3):
            rows = pl.ds(m(16 * ((x + d) % SIDE), 16), 16)
            group.push(gram_half.at[rows, cols], gram_one.at[0, d - 1, :, cols], at_x(d))
            rows = pl.ds(m(64 + 16 * ((y + d) % SIDE), 16), 16)
            group.push(gram_half.at[rows, cols], gram_one.at[1, d - 1, :, cols], at_y(d))
        return group

    def spread(cols, before):
        before.wait_recv()
        group = Group("spread", gram_half.at[pl.ds(0, 96), cols])
        for t in range(2):
            total = gram[own[t], cols]
            for d in range(3):
                total = total + gram_one[t, d, :, cols].astype(jnp.float32)
            gram_sum[t, :, cols] = total.astype(jnp.bfloat16)
        for d in (2, 1, 3):
            group.push(gram_sum.at[0, :, cols], gram_two.at[0, d - 1, :, cols], at_y(d))
            group.push(gram_sum.at[1, :, cols], gram_two.at[1, d - 1, :, cols], at_x(d))
        return group

    def collect(cols, before):
        before.wait_recv()
        group = Group("collect", gram_half.at[pl.ds(0, 96), cols])
        for t in range(2):
            total = gram_sum[t, :, cols].astype(jnp.float32)
            for d in range(3):
                total = total + gram_two[t, d, :, cols].astype(jnp.float32)
            gram_all[own[t], cols] = total.astype(jnp.bfloat16)
        for d in (2, 1, 3):
            ref = gram_all.at[own[0], cols]
            group.push(ref, ref, at_x(d))
            ref = gram_all.at[own[1], cols]
            group.push(ref, ref, at_y(d))
        return group

    def last_one():
        group = Group("last_one", gram_half.at[:, pl.ds(0, 3 * IMG)])
        for d in (2, 1, 3):
            group.push(gram_half.at[low, late], last_part.at[0, d - 1], at_x(d))
            group.push(gram_half.at[high, late], last_part.at[1, d - 1], at_y(d))
        return group

    def last_two(before):
        before.wait_recv()
        group = Group("last_two", gram_half.at[:, pl.ds(0, 3 * IMG)])
        for t, rows in enumerate((low, high)):
            total = gram_half[rows, late].astype(jnp.float32)
            for d in range(3):
                total = total + last_part[t, d].astype(jnp.float32)
            last_sum[t] = total.astype(jnp.bfloat16)
        for d in (2, 1, 3):
            group.push(last_sum.at[0], last_part.at[2, d - 1], at_y(d))
            group.push(last_sum.at[1], last_part.at[3, d - 1], at_x(d))
        return group

    def last_end(before):
        before.wait_recv()
        for t, rows in enumerate((low, high)):
            total = last_sum[t].astype(jnp.float32)
            for d in range(3):
                total = total + last_part[2 + t, d].astype(jnp.float32)
            gram_all[rows, late] = total.astype(jnp.bfloat16)

    for k in (0, 1, 7):
        center(k)
    parts = []

    def in_third():
        for k in (0, 1, 7):
            multiply(k)
        for k in (2, 6):
            center(k)
            multiply(k)
        parts.append(scatter(early))

    gather_step("emb", emb, 3, down, up, in_third)
    for k in (3, 5):
        center(k)
        multiply(k)
    parts.append(scatter(middle))
    parts[0] = spread(early, parts[0])
    down[0].wait_recv()
    up[1].wait_recv()
    center(4)
    multiply(4)
    final = last_one()
    parts[1] = spread(middle, parts[1])
    deviation = jnp.sqrt(
        jnp.sum(squares[0], 0, keepdims=True) / (IMAGES - 1) + variance_epsilon
    )
    dev_out[...] = deviation
    diagonal = jnp.sum(squares[1], 0, keepdims=True)
    parts[0] = collect(early, parts[0])
    final = last_two(final)
    parts[1] = collect(middle, parts[1])
    partner_copy.wait_recv()
    parts[0].wait_recv()
    before_last = pl.ds(0, EARLY)
    covariance_part = jnp.dot(
        gram_all[:, before_last], cen[before_last, :], preferred_element_type=jnp.float32
    )
    part[0] = covariance_part
    last_end(final)
    parts[1].wait_recv()

    coefficient = 4.0 * covariance_weight * LOSS_SCALE / (OUT * (IMAGES - 1)) / (IMAGES - 1)
    hinge_scale = jnp.where(deviation < 1.0, 1.0 / deviation, 0.0) * (
        LOSS_SCALE * variance_weight / (2.0 * OUT * (IMAGES - 1))
    )
    direct_scale = LOSS_SCALE * 2.0 * invariance_weight / (IMAGES * OUT)

    def gradient(rows):
        rest = pl.ds(EARLY, IMAGES - EARLY)
        covariance = part[0, rows, :] + jnp.dot(
            gram_all[rows, rest], cen[rest, :], preferred_element_type=jnp.float32
        )
        half = cen[rows, :].astype(jnp.float32)
        values = emb[rows, :].astype(jnp.float32)
        total = (
            direct_scale * (values - partner[rows, :].astype(jnp.float32))
            - hinge_scale * (values - mean_values)
            + coefficient * (covariance - half * diagonal)
        )
        grads[rows, :] = total.astype(jnp.bfloat16)

    down, up = start_gather("grads", grads, lambda rows, half: gradient(rows))

    def times(ks, cols):
        n = len(ks)
        left = feats[pl.ds(SLOT[ks[0]], n), :, cols].reshape(n * IMG, cols.size)
        right = grads[pl.ds(PLACE[ks[0]] * IMG, n * IMG), :]
        return transposed_product(left, right)

    acc[...] = times((0,), orows)
    mine[...] = times((0,), wrows)
    for step in range(1, 4):
        gather_step("grads", grads, step, down, up)
        acc[...] += times((step, N - step), orows)
        mine[...] += times((step, N - step), wrows)
    down[0].wait_recv()
    up[1].wait_recv()

    lasts = []
    for i in range(2):
        rows = pl.ds(i * 256, 256)
        product = times((4,), pl.ds(m((1 - v) * WIDTH + i * 256, 256), 256))
        give[rows, :] = (acc[rows, :] + product).astype(jnp.bfloat16)
        lasts.append(push("last", give.at[rows], theirs.at[rows], other))
    mine[...] += times((4,), wrows)
    five = pl.ds(1, 5)
    wait_sends("first", feats.at[five, pl.ds(0, 32), pl.ds(0, 256)])
    wait_sends("second", feats.at[five, pl.ds(0, 96), pl.ds(0, 256)])
    wait_sends("third", feats.at[five, pl.ds(0, 96), :])
    wait_sends("near", feats.at[slots((1, 7))])
    wait_sends("weight", weight)
    wait_sends("reduce", emb.at[pl.ds(0, 7 * IMG)])
    wait_sends("emb", emb.at[pl.ds(0, 7 * IMG)])
    wait_sends("grads", emb.at[pl.ds(0, 7 * IMG)])
    wait_sends("shares", sums.at[pl.ds(0, N - 1)])
    wait_sends("partner", partner)
    for name in ("scatter", "spread", "collect"):
        wait_sends(name, gram_half.at[pl.ds(0, 96), pl.ds(0, LATE)])
    for name in ("last_one", "last_two"):
        wait_sends(name, gram_half.at[:, pl.ds(0, 3 * IMG)])
    for i in range(2):
        rows = pl.ds(i * 256, 256)
        lasts[i].wait_recv()
        grad_out[rows, :] = mine[rows, :] + theirs[rows, :].astype(jnp.float32)
    wait_sends("last", give)
    assert not sends and len(groups) <= WAITS


def per_device(hidden, weight):
    vmem = pl.BlockSpec(memory_space=pltpu.VMEM)
    hbm = pl.BlockSpec(memory_space=pltpu.HBM)
    half, full = jnp.bfloat16, jnp.float32
    return pl.pallas_call(
        kernel,
        out_shape=(
            jax.ShapeDtypeStruct((1, IMG, WIDTH), half),
            jax.ShapeDtypeStruct((WIDTH, WIDTH), full),
            jax.ShapeDtypeStruct((1, WIDTH), full),
        ),
        in_specs=[hbm, hbm],
        out_specs=(vmem, vmem, vmem),
        scratch_shapes=[
            pltpu.VMEM((IMG, OUT), half),
            pltpu.VMEM((N, IMG, 2 * WIDTH), half),
            pltpu.VMEM((2 * WIDTH, WIDTH), half),
            pltpu.VMEM((N, IMG, WIDTH), full),
            pltpu.VMEM((2, 4, 2, 64, WIDTH), half),
            pltpu.VMEM((2, 4, 2, 64, WIDTH), half),
            pltpu.VMEM((IMAGES, WIDTH), half),
            pltpu.VMEM((IMAGES, WIDTH), half),
            pltpu.VMEM((IMG, WIDTH), half),
            pltpu.VMEM((N, 1, WIDTH), full),
            pltpu.VMEM((2, N, WIDTH), full),
            pltpu.VMEM((IMG, IMAGES), full),
            pltpu.VMEM((IMG, IMAGES), half),
            pltpu.VMEM((2, 3, 16, IMAGES), half),
            pltpu.VMEM((2, 16, IMAGES), half),
            pltpu.VMEM((2, 3, 16, IMAGES), half),
            pltpu.VMEM((4, 3, 64, IMG), half),
            pltpu.VMEM((2, 64, IMG), half),
            pltpu.VMEM((IMG, IMAGES), half),
            pltpu.VMEM((IMAGES, WIDTH), half),
            pltpu.VMEM((WIDTH, WIDTH), full),
            pltpu.VMEM((WIDTH, WIDTH), full),
            pltpu.VMEM((WIDTH, WIDTH), half),
            pltpu.VMEM((WIDTH, WIDTH), half),
            pltpu.SemaphoreType.DMA((2,)),
            pltpu.SemaphoreType.DMA((SENDS,)),
            pltpu.SemaphoreType.DMA((WAITS,)),
        ],
        compiler_params=pltpu.CompilerParams(
            collective_id=0, has_side_effects=True, vmem_limit_bytes=52 << 20
        ),
        name="expander",
    )(hidden, weight)


def solution(mesh):
    placed = (P("view", "dp", None), P(("view", "dp"), "unit"))
    return jax.shard_map(
        per_device,
        mesh=mesh,
        in_specs=placed,
        out_specs=(P("view", "dp", "unit"), P(("view", "dp"), "unit"), P("view", "unit")),
        check_vma=False,
    )
```

```python
import jax
import jax.numpy as jnp
from jax import lax
from jax.experimental import pallas as pl
from jax.experimental.pallas import tpu as pltpu
from jax.sharding import PartitionSpec as P

invariance_weight = 25.0
variance_weight = 25.0
covariance_weight = 1.0
variance_epsilon = 0.0001

IMG = 128
N = 8
SIDE = 4
WIDTH = 512
OUT = 8192
IMAGES = IMG * N
LOSS_SCALE = IMAGES * OUT / 4096.0
SLOT = {0: 0, 4: 1, 3: 2, 5: 3, 2: 4, 6: 5, 1: 6, 7: 7}
PLACE = {0: 0, 1: 1, 7: 2, 2: 3, 6: 4, 3: 5, 5: 6, 4: 7}
GROUPS = ((4,), (3, 5), (2, 6))
EARLY, LATE = 5 * IMG, 7 * IMG
WAITS = 72
SENDS = 20


def transposed_product(left, right):
    return lax.dot_general(
        left, right, (((0,), (0,)), ((), ())), preferred_element_type=jnp.float32
    )


def product_transposed(left, right):
    return lax.dot_general(
        left, right, (((1,), (1,)), ((), ())), preferred_element_type=jnp.float32
    )


def kernel(
    hidden,
    weight,
    emb_out,
    grad_out,
    dev_out,
    held,
    feats,
    wgt,
    part,
    far_send,
    far_recv,
    red_send,
    red_recv,
    emb,
    cen,
    partner,
    sums,
    squares,
    gram,
    gram_half,
    gram_one,
    gram_sum,
    gram_two,
    last_part,
    last_sum,
    gram_all,
    grads,
    acc,
    mine,
    give,
    theirs,
    local_sem,
    send_sem,
    recv_sem,
):
    v, j, u = lax.axis_index("view"), lax.axis_index("dp"), lax.axis_index("unit")
    x, y = u // SIDE, u % SIDE

    def at_z(k):
        return (v, (j + k + N) % N, u)

    def at_x(d):
        return (v, j, ((x + d) % SIDE) * SIDE + y)

    def at_y(d):
        return (v, j, x * SIDE + (y + d) % SIDE)

    other = (1 - v, j, u)
    groups, sends = [], {}

    class Group:
        def __init__(self, name, like):
            self.at, self.name, self.like = len(groups), name, like
            groups.append(self)
            sends.setdefault(name, len(sends))

        def push(self, src, dst, device):
            pltpu.make_async_remote_copy(
                src_ref=src,
                dst_ref=dst,
                send_sem=send_sem.at[sends[self.name]],
                recv_sem=recv_sem.at[self.at],
                device_id=device,
                device_id_type=pl.DeviceIdType.MESH,
            ).start()

        def wait_recv(self):
            pltpu.make_async_copy(self.like, self.like, recv_sem.at[self.at]).wait()

    def push(name, src, dst, device):
        group = Group(name, src)
        group.push(src, dst, device)
        return group

    def wait_sends(name, like):
        pltpu.make_async_copy(like, like, send_sem.at[sends.pop(name)]).wait()

    def m(value, by):
        return pl.multiple_of(value, by)

    def slots(group):
        return pl.ds(SLOT[group[0]], len(group))

    wrows = pl.ds(m(v * WIDTH, WIDTH), WIDTH)
    orows = pl.ds(m((1 - v) * WIDTH, WIDTH), WIDTH)
    load_hidden = pltpu.make_async_copy(hidden.at[0], held, local_sem.at[0])
    load_weight = pltpu.make_async_copy(weight, wgt.at[wrows], local_sem.at[1])
    load_hidden.start()
    load_weight.start()

    def columns_of(block, c):
        return pl.ds(m(c * (OUT // 2) + block * WIDTH, WIDTH), WIDTH)

    barrier = pltpu.get_barrier_semaphore()
    peers = [at_z(k) for k in range(1, N)]
    peers += [at_x(d) for d in range(1, SIDE)] + [at_y(d) for d in range(1, SIDE)] + [other]
    for peer in peers:
        pl.semaphore_signal(barrier, inc=1, device_id=peer, device_id_type=pl.DeviceIdType.MESH)
    pl.semaphore_wait(barrier, len(peers))

    a_rows, a_cols = pl.ds(m(16 * y, 16), 16), pl.ds(m(256 * x, 256), 256)
    b_rows, b_cols = pl.ds(m(64 + 16 * x, 16), 16), pl.ds(m(256 * y, 256), 256)
    load_hidden.wait()
    first = []
    for group in GROUPS:
        first.append(Group("first", feats.at[slots(group), pl.ds(0, 32), pl.ds(0, 256)]))
        for k in group:
            to = (j - k + N) % N
            a_from = pl.ds(m((x // 2) * (OUT // 2) + to * WIDTH + (x % 2) * 256, 256), 256)
            b_from = pl.ds(m((y // 2) * (OUT // 2) + to * WIDTH + (y % 2) * 256, 256), 256)
            a_to, b_to = feats.at[SLOT[k], a_rows, a_cols], feats.at[SLOT[k], b_rows, b_cols]
            first[-1].push(held.at[a_rows, a_from], a_to, at_z(-k))
            first[-1].push(held.at[b_rows, b_from], b_to, at_z(-k))
        if group == (4,):
            load_weight.wait()
            weight_copy = push("weight", wgt.at[wrows], wgt.at[wrows], other)

    def project(k):
        part[SLOT[k]] = jnp.dot(feats[SLOT[k]], wgt[...], preferred_element_type=jnp.float32)


    second, third = [], []

    def along_one(g):
        group = GROUPS[g]
        first[g].wait_recv()
        a = feats.at[slots(group), a_rows, a_cols]
        b = feats.at[slots(group), b_rows, b_cols]
        second.append(Group("second", feats.at[slots(group), pl.ds(0, 96), pl.ds(0, 256)]))
        for d in (2, 1, 3):
            second[g].push(a, a, at_x(d))
            second[g].push(b, b, at_y(d))

    def along_both(g):
        group = GROUPS[g]
        second[g].wait_recv()
        a = feats.at[slots(group), a_rows, :]
        b = feats.at[slots(group), b_rows, :]
        third.append(Group("third", feats.at[slots(group), pl.ds(0, 96), :]))
        for d in (2, 1, 3):
            third[g].push(a, a, at_y(d))
            third[g].push(b, b, at_x(d))

    def take(g):
        third[g].wait_recv()

    low, high = pl.ds(0, 64), pl.ds(64, 64)

    def reduce_far(way, half):
        rows, cols = pl.ds(64 * half, 64), pl.ds(256 * way, 256)
        far_send[way, half] = part[SLOT[4], rows, cols].astype(jnp.bfloat16)
        return push(
            "far", far_send.at[way, half], far_recv.at[way, half], at_z(-2 if way == 0 else 2)
        )

    def reduce_on(way, step, k, half, before=None, far=None):
        rows, cols = pl.ds(64 * half, 64), pl.ds(256 * way, 256)
        total = part[SLOT[k], rows, :]
        if before is not None:
            before.wait_recv()
            total = total + red_recv[way, step - 1, half].astype(jnp.float32)
        red_send[way, step, half] = total.astype(jnp.bfloat16)
        if far is not None:
            far.wait_recv()
            total = total[:, 256 * way : 256 * way + 256]
            total = total + far_recv[way, half].astype(jnp.float32)
            red_send[way, step, half, :, cols] = total.astype(jnp.bfloat16)
        return push(
            "reduce",
            red_send.at[way, step, half],
            red_recv.at[way, step, half],
            at_z(-1 if way == 0 else 1),
        )

    along_one(0)
    along_one(1)
    near = Group("near", feats.at[slots((1, 7))])
    for c in range(2):
        for k in (1, 7):
            to = (j - k + N) % N
            at = feats.at[SLOT[k], :, pl.ds(c * WIDTH, WIDTH)]
            near.push(held.at[:, columns_of(to, c)], at, at_z(-k))
    along_one(2)
    along_both(0)
    along_both(1)
    for c in range(2):
        feats[0, :, pl.ds(c * WIDTH, WIDTH)] = held[:, columns_of(j, c)]
    weight_copy.wait_recv()
    project(0)
    take(0)
    project(4)
    far = [[reduce_far(way, half) for way in range(2)] for half in range(2)]
    along_both(2)
    take(1)
    running = [[None, None], [None, None]]
    for step in range(3):
        for way, k in ((0, 5 + step), (1, 3 - step)):
            project(k)
            if step == 0:
                running[0][way] = reduce_on(way, 0, k, 0)
        for half in range(2):
            for way, k in ((0, 5 + step), (1, 3 - step)):
                if step == 0 and half == 0:
                    continue
                running[half][way] = reduce_on(
                    way,
                    step,
                    k,
                    half,
                    running[half][way],
                    far[half][way] if step == 1 else None,
                )
        if step == 0:
            take(2)
        if step == 1:
            near.wait_recv()

    def finish(rows, half):
        total = part[0, rows, :] + (
            red_recv[0, 2, half].astype(jnp.float32) + red_recv[1, 2, half].astype(jnp.float32)
        )
        emb[rows, :] = total.astype(jnp.bfloat16)

    def block(k):
        return pl.ds(PLACE[k] * IMG, IMG)

    def half_block(k, h):
        return pl.ds(PLACE[k] * IMG + 64 * h, 64)

    def start_gather(name, buf, make):
        down, up = [None, None], [None, None]
        for h, rows in enumerate((low, high)):
            make(rows, h)
            down[h] = push(name, buf.at[half_block(0, h)], buf.at[half_block(1, h)], at_z(-1))
            up[h] = push(name, buf.at[half_block(0, h)], buf.at[half_block(7, h)], at_z(1))
        return down, up

    def gather_step(name, buf, step, down, up, between=None):
        far = None
        if step == 2:
            far = Group(name + "_far", buf.at[pl.ds(0, IMG)])
        for h in (0, 1):
            for ways, way, at, to in ((down, 0, step, step + 1), (up, 1, N - step, N - step - 1)):
                ways[h].wait_recv()
                if step < 3:
                    ways[h] = push(
                        name,
                        buf.at[half_block(at, h)],
                        buf.at[half_block(to, h)],
                        at_z(-1 if way == 0 else 1),
                    )
                if step == 2:
                    for i in (h,):
                        cols = pl.ds(256 * way, 256)
                        far.push(
                            buf.at[half_block(at, i), cols],
                            buf.at[half_block(4, i), cols],
                            at_z(-2 if way == 0 else 2),
                        )
            if h == 0 and between is not None:
                between()
        return far

    def reduced(rows, half):
        for way in range(2):
            running[half][way].wait_recv()
        finish(rows, half)

    down, up = start_gather("emb", emb, reduced)
    sums[pl.ds(j, 1)] = jnp.sum(emb[block(0), :].astype(jnp.float32), 0, keepdims=True)[None]
    shares = Group("shares", sums.at[pl.ds(0, N - 1)])
    for k in (4, 3, 5, 2, 6, 1, 7):
        shares.push(sums.at[pl.ds(j, 1)], sums.at[pl.ds(j, 1)], at_z(k))
    partner_copy = push("partner", emb.at[block(0)], partner, other)
    emb_out[0] = emb[block(0), :]

    gather_step("emb", emb, 1, down, up)
    last_block = gather_step("emb", emb, 2, down, up)
    shares.wait_recv()
    mean_values = jnp.sum(sums[...], 0) / IMAGES

    def center(k):
        centered = emb[block(k), :].astype(jnp.float32) - mean_values
        half = centered.astype(jnp.bfloat16)
        cen[block(k), :] = half
        half = half.astype(jnp.float32)
        squares[0, pl.ds((j + k) % N, 1), :] = jnp.sum(centered * centered, 0, keepdims=True)
        squares[1, pl.ds((j + k) % N, 1), :] = jnp.sum(half * half, 0, keepdims=True)

    def multiply(k):
        product = product_transposed(cen[block(0), :], cen[block(k), :])
        gram[:, block(k)] = product
        gram_half[:, block(k)] = product.astype(jnp.bfloat16)

    own = (pl.ds(m(16 * x, 16), 16), pl.ds(m(64 + 16 * y, 16), 16))
    early, middle, late = pl.ds(0, EARLY), pl.ds(EARLY, LATE - EARLY), pl.ds(LATE, IMG)

    def scatter(cols):
        group = Group("scatter", gram_half.at[pl.ds(0, 96), cols])
        for d in (2, 1, 3):
            rows = pl.ds(m(16 * ((x + d) % SIDE), 16), 16)
            group.push(gram_half.at[rows, cols], gram_one.at[0, d - 1, :, cols], at_x(d))
            rows = pl.ds(m(64 + 16 * ((y + d) % SIDE), 16), 16)
            group.push(gram_half.at[rows, cols], gram_one.at[1, d - 1, :, cols], at_y(d))
        return group

    def spread(cols, before):
        before.wait_recv()
        group = Group("spread", gram_half.at[pl.ds(0, 96), cols])
        for t in range(2):
            total = gram[own[t], cols]
            for d in range(3):
                total = total + gram_one[t, d, :, cols].astype(jnp.float32)
            gram_sum[t, :, cols] = total.astype(jnp.bfloat16)
        for d in (2, 1, 3):
            group.push(gram_sum.at[0, :, cols], gram_two.at[0, d - 1, :, cols], at_y(d))
            group.push(gram_sum.at[1, :, cols], gram_two.at[1, d - 1, :, cols], at_x(d))
        return group

    def collect(cols, before):
        before.wait_recv()
        group = Group("collect", gram_half.at[pl.ds(0, 96), cols])
        for t in range(2):
            total = gram_sum[t, :, cols].astype(jnp.float32)
            for d in range(3):
                total = total + gram_two[t, d, :, cols].astype(jnp.float32)
            gram_all[own[t], cols] = total.astype(jnp.bfloat16)
        for d in (2, 1, 3):
            ref = gram_all.at[own[0], cols]
            group.push(ref, ref, at_x(d))
            ref = gram_all.at[own[1], cols]
            group.push(ref, ref, at_y(d))
        return group

    def last_one():
        group = Group("last_one", gram_half.at[:, pl.ds(0, 3 * IMG)])
        for d in (2, 1, 3):
            group.push(gram_half.at[low, late], last_part.at[0, d - 1], at_x(d))
            group.push(gram_half.at[high, late], last_part.at[1, d - 1], at_y(d))
        return group

    def last_two(before):
        before.wait_recv()
        group = Group("last_two", gram_half.at[:, pl.ds(0, 3 * IMG)])
        for t, rows in enumerate((low, high)):
            total = gram_half[rows, late].astype(jnp.float32)
            for d in range(3):
                total = total + last_part[t, d].astype(jnp.float32)
            last_sum[t] = total.astype(jnp.bfloat16)
        for d in (2, 1, 3):
            group.push(last_sum.at[0], last_part.at[2, d - 1], at_y(d))
            group.push(last_sum.at[1], last_part.at[3, d - 1], at_x(d))
        return group

    def last_end(before):
        before.wait_recv()
        for t, rows in enumerate((low, high)):
            total = last_sum[t].astype(jnp.float32)
            for d in range(3):
                total = total + last_part[2 + t, d].astype(jnp.float32)
            gram_all[rows, late] = total.astype(jnp.bfloat16)

    for k in (0, 1, 7):
        center(k)
    parts = []

    def in_third():
        for k in (0, 1, 7):
            multiply(k)
        for k in (2, 6):
            center(k)
            multiply(k)
        parts.append(scatter(early))

    gather_step("emb", emb, 3, down, up, in_third)
    for k in (3, 5):
        center(k)
        multiply(k)
    parts.append(scatter(middle))
    parts[0] = spread(early, parts[0])
    last_block.wait_recv()
    center(4)
    multiply(4)
    final = last_one()
    parts[1] = spread(middle, parts[1])
    deviation = jnp.sqrt(
        jnp.sum(squares[0], 0, keepdims=True) / (IMAGES - 1) + variance_epsilon
    )
    dev_out[...] = deviation
    diagonal = jnp.sum(squares[1], 0, keepdims=True)
    parts[0] = collect(early, parts[0])
    final = last_two(final)
    parts[1] = collect(middle, parts[1])
    partner_copy.wait_recv()
    parts[0].wait_recv()
    before_last = pl.ds(0, EARLY)
    covariance_part = jnp.dot(
        gram_all[:, before_last], cen[before_last, :], preferred_element_type=jnp.float32
    )
    part[0] = covariance_part
    last_end(final)
    parts[1].wait_recv()

    coefficient = 4.0 * covariance_weight * LOSS_SCALE / (OUT * (IMAGES - 1)) / (IMAGES - 1)
    hinge_scale = jnp.where(deviation < 1.0, 1.0 / deviation, 0.0) * (
        LOSS_SCALE * variance_weight / (2.0 * OUT * (IMAGES - 1))
    )
    direct_scale = LOSS_SCALE * 2.0 * invariance_weight / (IMAGES * OUT)

    def gradient(rows):
        rest = pl.ds(EARLY, IMAGES - EARLY)
        covariance = part[0, rows, :] + jnp.dot(
            gram_all[rows, rest], cen[rest, :], preferred_element_type=jnp.float32
        )
        half = cen[rows, :].astype(jnp.float32)
        values = emb[rows, :].astype(jnp.float32)
        total = (
            direct_scale * (values - partner[rows, :].astype(jnp.float32))
            - hinge_scale * (values - mean_values)
            + coefficient * (covariance - half * diagonal)
        )
        grads[rows, :] = total.astype(jnp.bfloat16)

    down, up = start_gather("grads", grads, lambda rows, half: gradient(rows))

    def times(ks, cols):
        n = len(ks)
        left = feats[pl.ds(SLOT[ks[0]], n), :, cols].reshape(n * IMG, cols.size)
        right = grads[pl.ds(PLACE[ks[0]] * IMG, n * IMG), :]
        return transposed_product(left, right)

    acc[...] = times((0,), orows)
    mine[...] = times((0,), wrows)
    for step in range(1, 3):
        last_block = gather_step("grads", grads, step, down, up)
        acc[...] += times((step, N - step), orows)
        mine[...] += times((step, N - step), wrows)
    gather_step("grads", grads, 3, down, up)
    acc[...] += times((3, 5), orows)
    last_block.wait_recv()
    lasts = []
    for i in range(2):
        rows = pl.ds(i * 256, 256)
        product = times((4,), pl.ds(m((1 - v) * WIDTH + i * 256, 256), 256))
        give[rows, :] = (acc[rows, :] + product).astype(jnp.bfloat16)
        lasts.append(push("last", give.at[rows], theirs.at[rows], other))
    mine[...] += times((3, 5), wrows) + times((4,), wrows)
    five = pl.ds(1, 5)
    wait_sends("first", feats.at[five, pl.ds(0, 32), pl.ds(0, 256)])
    wait_sends("second", feats.at[five, pl.ds(0, 96), pl.ds(0, 256)])
    wait_sends("third", feats.at[five, pl.ds(0, 96), :])
    wait_sends("near", feats.at[slots((1, 7))])
    wait_sends("weight", weight)
    wait_sends("far", partner)
    for name in ("reduce", "emb", "grads"):
        wait_sends(name, emb.at[pl.ds(0, 6 * IMG)])
    for name in ("emb_far", "grads_far"):
        wait_sends(name, partner)
    wait_sends("shares", sums.at[pl.ds(0, N - 1)])
    wait_sends("partner", partner)
    for name in ("scatter", "spread", "collect"):
        wait_sends(name, gram_half.at[pl.ds(0, 96), pl.ds(0, LATE)])
    for name in ("last_one", "last_two"):
        wait_sends(name, gram_half.at[:, pl.ds(0, 3 * IMG)])
    for i in range(2):
        rows = pl.ds(i * 256, 256)
        lasts[i].wait_recv()
        grad_out[rows, :] = mine[rows, :] + theirs[rows, :].astype(jnp.float32)
    wait_sends("last", give)
    assert not sends and len(groups) <= WAITS


def per_device(hidden, weight):
    vmem = pl.BlockSpec(memory_space=pltpu.VMEM)
    hbm = pl.BlockSpec(memory_space=pltpu.HBM)
    half, full = jnp.bfloat16, jnp.float32
    return pl.pallas_call(
        kernel,
        out_shape=(
            jax.ShapeDtypeStruct((1, IMG, WIDTH), half),
            jax.ShapeDtypeStruct((WIDTH, WIDTH), full),
            jax.ShapeDtypeStruct((1, WIDTH), full),
        ),
        in_specs=[hbm, hbm],
        out_specs=(vmem, vmem, vmem),
        scratch_shapes=[
            pltpu.VMEM((IMG, OUT), half),
            pltpu.VMEM((N, IMG, 2 * WIDTH), half),
            pltpu.VMEM((2 * WIDTH, WIDTH), half),
            pltpu.VMEM((N, IMG, WIDTH), full),
            pltpu.VMEM((2, 2, 64, 256), half),
            pltpu.VMEM((2, 2, 64, 256), half),
            pltpu.VMEM((2, 3, 2, 64, WIDTH), half),
            pltpu.VMEM((2, 3, 2, 64, WIDTH), half),
            pltpu.VMEM((IMAGES, WIDTH), half),
            pltpu.VMEM((IMAGES, WIDTH), half),
            pltpu.VMEM((IMG, WIDTH), half),
            pltpu.VMEM((N, 1, WIDTH), full),
            pltpu.VMEM((2, N, WIDTH), full),
            pltpu.VMEM((IMG, IMAGES), full),
            pltpu.VMEM((IMG, IMAGES), half),
            pltpu.VMEM((2, 3, 16, IMAGES), half),
            pltpu.VMEM((2, 16, IMAGES), half),
            pltpu.VMEM((2, 3, 16, IMAGES), half),
            pltpu.VMEM((4, 3, 64, IMG), half),
            pltpu.VMEM((2, 64, IMG), half),
            pltpu.VMEM((IMG, IMAGES), half),
            pltpu.VMEM((IMAGES, WIDTH), half),
            pltpu.VMEM((WIDTH, WIDTH), full),
            pltpu.VMEM((WIDTH, WIDTH), full),
            pltpu.VMEM((WIDTH, WIDTH), half),
            pltpu.VMEM((WIDTH, WIDTH), half),
            pltpu.SemaphoreType.DMA((2,)),
            pltpu.SemaphoreType.DMA((SENDS,)),
            pltpu.SemaphoreType.DMA((WAITS,)),
        ],
        compiler_params=pltpu.CompilerParams(
            collective_id=0, has_side_effects=True, vmem_limit_bytes=52 << 20
        ),
        name="expander",
    )(hidden, weight)


def solution(mesh):
    placed = (P("view", "dp", None), P(("view", "dp"), "unit"))
    return jax.shard_map(
        per_device,
        mesh=mesh,
        in_specs=placed,
        out_specs=(P("view", "dp", "unit"), P(("view", "dp"), "unit"), P("view", "unit")),
        check_vma=False,
    )
```

```python
import jax
import jax.numpy as jnp
from jax import lax
from jax.experimental import pallas as pl
from jax.experimental.pallas import tpu as pltpu
from jax.sharding import PartitionSpec as P

invariance_weight = 25.0
variance_weight = 25.0
covariance_weight = 1.0
variance_epsilon = 0.0001

IMG = 128
N = 8
SIDE = 4
WIDTH = 512
OUT = 8192
IMAGES = IMG * N
LOSS_SCALE = IMAGES * OUT / 4096.0
SLOT = {0: 0, 4: 1, 3: 2, 5: 3, 2: 4, 6: 5, 1: 6, 7: 7}
PLACE = {0: 0, 1: 1, 7: 2, 2: 3, 6: 4, 3: 5, 5: 6, 4: 7}
GROUPS = ((4,), (3, 5), (2, 6))
EARLY, LATE = 5 * IMG, 7 * IMG
PARTS = 4
ROWS = IMG // PARTS
WAITS = 105
SENDS = 19


def transposed_product(left, right):
    return lax.dot_general(
        left, right, (((0,), (0,)), ((), ())), preferred_element_type=jnp.float32
    )


def product_transposed(left, right):
    return lax.dot_general(
        left, right, (((1,), (1,)), ((), ())), preferred_element_type=jnp.float32
    )


def kernel(
    hidden,
    weight,
    emb_out,
    grad_out,
    dev_out,
    held,
    feats,
    wgt,
    part,
    far_send,
    far_recv,
    red_send,
    red_recv,
    emb,
    cen,
    partner,
    sums,
    squares,
    gram,
    gram_half,
    gram_one,
    gram_sum,
    gram_two,
    last_part,
    last_sum,
    gram_all,
    grads,
    acc,
    mine,
    give,
    theirs,
    local_sem,
    send_sem,
    recv_sem,
):
    v, j, u = lax.axis_index("view"), lax.axis_index("dp"), lax.axis_index("unit")
    x, y = u // SIDE, u % SIDE

    def at_z(k):
        return (v, (j + k + N) % N, u)

    def at_x(d):
        return (v, j, ((x + d) % SIDE) * SIDE + y)

    def at_y(d):
        return (v, j, x * SIDE + (y + d) % SIDE)

    other = (1 - v, j, u)
    groups, sends = [], {}

    class Group:
        def __init__(self, name, like):
            self.at, self.name, self.like = len(groups), name, like
            groups.append(self)
            sends.setdefault(name, len(sends))

        def push(self, src, dst, device):
            pltpu.make_async_remote_copy(
                src_ref=src,
                dst_ref=dst,
                send_sem=send_sem.at[sends[self.name]],
                recv_sem=recv_sem.at[self.at],
                device_id=device,
                device_id_type=pl.DeviceIdType.MESH,
            ).start()

        def wait_recv(self):
            pltpu.make_async_copy(self.like, self.like, recv_sem.at[self.at]).wait()

    def push(name, src, dst, device):
        group = Group(name, src)
        group.push(src, dst, device)
        return group

    def wait_sends(name, like):
        pltpu.make_async_copy(like, like, send_sem.at[sends.pop(name)]).wait()

    def m(value, by):
        return pl.multiple_of(value, by)

    def slots(group):
        return pl.ds(SLOT[group[0]], len(group))

    wrows = pl.ds(m(v * WIDTH, WIDTH), WIDTH)
    orows = pl.ds(m((1 - v) * WIDTH, WIDTH), WIDTH)
    load_hidden = pltpu.make_async_copy(hidden.at[0], held, local_sem.at[0])
    load_weight = pltpu.make_async_copy(weight, wgt.at[wrows], local_sem.at[1])
    load_hidden.start()
    load_weight.start()

    def columns_of(block, c):
        return pl.ds(m(c * (OUT // 2) + block * WIDTH, WIDTH), WIDTH)

    barrier = pltpu.get_barrier_semaphore()
    peers = [at_z(k) for k in range(1, N)]
    peers += [at_x(d) for d in range(1, SIDE)] + [at_y(d) for d in range(1, SIDE)] + [other]
    for peer in peers:
        pl.semaphore_signal(barrier, inc=1, device_id=peer, device_id_type=pl.DeviceIdType.MESH)
    pl.semaphore_wait(barrier, len(peers))

    a_rows, a_cols = pl.ds(m(16 * y, 16), 16), pl.ds(m(256 * x, 256), 256)
    b_rows, b_cols = pl.ds(m(64 + 16 * x, 16), 16), pl.ds(m(256 * y, 256), 256)
    load_hidden.wait()
    first = []
    for group in GROUPS:
        first.append(Group("first", feats.at[slots(group), pl.ds(0, 32), pl.ds(0, 256)]))
        for k in group:
            to = (j - k + N) % N
            a_from = pl.ds(m((x // 2) * (OUT // 2) + to * WIDTH + (x % 2) * 256, 256), 256)
            b_from = pl.ds(m((y // 2) * (OUT // 2) + to * WIDTH + (y % 2) * 256, 256), 256)
            a_to, b_to = feats.at[SLOT[k], a_rows, a_cols], feats.at[SLOT[k], b_rows, b_cols]
            first[-1].push(held.at[a_rows, a_from], a_to, at_z(-k))
            first[-1].push(held.at[b_rows, b_from], b_to, at_z(-k))
        if group == (4,):
            load_weight.wait()
            weight_copy = push("weight", wgt.at[wrows], wgt.at[wrows], other)

    def project(k):
        part[SLOT[k]] = jnp.dot(feats[SLOT[k]], wgt[...], preferred_element_type=jnp.float32)


    second, third = [], []

    def along_one(g):
        group = GROUPS[g]
        first[g].wait_recv()
        a = feats.at[slots(group), a_rows, a_cols]
        b = feats.at[slots(group), b_rows, b_cols]
        second.append(Group("second", feats.at[slots(group), pl.ds(0, 96), pl.ds(0, 256)]))
        for d in (2, 1, 3):
            second[g].push(a, a, at_x(d))
            second[g].push(b, b, at_y(d))

    def along_both(g):
        group = GROUPS[g]
        second[g].wait_recv()
        a = feats.at[slots(group), a_rows, :]
        b = feats.at[slots(group), b_rows, :]
        third.append(Group("third", feats.at[slots(group), pl.ds(0, 96), :]))
        for d in (2, 1, 3):
            third[g].push(a, a, at_y(d))
            third[g].push(b, b, at_x(d))

    def take(g):
        third[g].wait_recv()

    low, high = pl.ds(0, 64), pl.ds(64, 64)

    def reduce_far(way, c):
        rows, cols = pl.ds(ROWS * c, ROWS), pl.ds(256 * way, 256)
        far_send[way, c] = part[SLOT[4], rows, cols].astype(jnp.bfloat16)
        return push(
            "far", far_send.at[way, c], far_recv.at[way, c], at_z(-2 if way == 0 else 2)
        )

    def reduce_on(way, step, k, c, before=None, far=None):
        rows, cols = pl.ds(ROWS * c, ROWS), pl.ds(256 * way, 256)
        total = part[SLOT[k], rows, :]
        if before is not None:
            before.wait_recv()
            total = total + red_recv[way, step - 1, c].astype(jnp.float32)
        red_send[way, step, c] = total.astype(jnp.bfloat16)
        if far is not None:
            far.wait_recv()
            total = total[:, 256 * way : 256 * way + 256]
            total = total + far_recv[way, c].astype(jnp.float32)
            red_send[way, step, c, :, cols] = total.astype(jnp.bfloat16)
        return push(
            "reduce",
            red_send.at[way, step, c],
            red_recv.at[way, step, c],
            at_z(-1 if way == 0 else 1),
        )

    along_one(0)
    along_one(1)
    near = Group("near", feats.at[slots((1, 7))])
    for c in range(2):
        for k in (1, 7):
            to = (j - k + N) % N
            at = feats.at[SLOT[k], :, pl.ds(c * WIDTH, WIDTH)]
            near.push(held.at[:, columns_of(to, c)], at, at_z(-k))
    along_one(2)
    along_both(0)
    along_both(1)
    for c in range(2):
        feats[0, :, pl.ds(c * WIDTH, WIDTH)] = held[:, columns_of(j, c)]
    weight_copy.wait_recv()
    project(0)
    take(0)
    project(4)
    far = [[reduce_far(way, c) for way in range(2)] for c in range(PARTS)]
    along_both(2)
    take(1)
    running = [[None, None] for c in range(PARTS)]
    for step in range(3):
        for way, k in ((0, 5 + step), (1, 3 - step)):
            project(k)
            if step == 0:
                running[0][way] = reduce_on(way, 0, k, 0)
        for c in range(PARTS):
            for way, k in ((0, 5 + step), (1, 3 - step)):
                if step == 0 and c == 0:
                    continue
                running[c][way] = reduce_on(
                    way, step, k, c, running[c][way], far[c][way] if step == 1 else None
                )
        if step == 0:
            take(2)
        if step == 1:
            near.wait_recv()

    def finish(c):
        rows = pl.ds(ROWS * c, ROWS)
        total = part[0, rows, :] + (
            red_recv[0, 2, c].astype(jnp.float32) + red_recv[1, 2, c].astype(jnp.float32)
        )
        emb[rows, :] = total.astype(jnp.bfloat16)

    def block(k):
        return pl.ds(PLACE[k] * IMG, IMG)

    def chunk(k, c):
        return pl.ds(PLACE[k] * IMG + ROWS * c, ROWS)

    def start_gather(name, buf, make):
        down, up = [], []
        for c in range(PARTS):
            make(c)
            down.append(push(name, buf.at[chunk(0, c)], buf.at[chunk(1, c)], at_z(-1)))
            up.append(push(name, buf.at[chunk(0, c)], buf.at[chunk(7, c)], at_z(1)))
        return down, up

    def gather_step(name, buf, step, down, up, between=None):
        far = None
        if step == 2:
            far = Group(name + "_far", buf.at[pl.ds(0, IMG)])
        for h in range(PARTS):
            for ways, way, at, to in ((down, 0, step, step + 1), (up, 1, N - step, N - step - 1)):
                ways[h].wait_recv()
                if step < 3:
                    ways[h] = push(
                        name,
                        buf.at[chunk(at, h)],
                        buf.at[chunk(to, h)],
                        at_z(-1 if way == 0 else 1),
                    )
                if step == 2:
                    for i in (h,):
                        cols = pl.ds(256 * way, 256)
                        far.push(
                            buf.at[chunk(at, i), cols],
                            buf.at[chunk(4, i), cols],
                            at_z(-2 if way == 0 else 2),
                        )
            if h == 0 and between is not None:
                between()
        return far

    def reduced(c):
        for way in range(2):
            running[c][way].wait_recv()
        finish(c)

    down, up = start_gather("emb", emb, reduced)
    sums[pl.ds(j, 1)] = jnp.sum(emb[block(0), :].astype(jnp.float32), 0, keepdims=True)[None]
    shares = Group("shares", sums.at[pl.ds(0, N - 1)])
    for k in (4, 3, 5, 2, 6, 1, 7):
        shares.push(sums.at[pl.ds(j, 1)], sums.at[pl.ds(j, 1)], at_z(k))
    partner_copy = push("partner", emb.at[block(0)], partner, other)
    emb_out[0] = emb[block(0), :]

    gather_step("emb", emb, 1, down, up)
    last_block = gather_step("emb", emb, 2, down, up)
    shares.wait_recv()
    mean_values = jnp.sum(sums[...], 0) / IMAGES

    def center(k):
        centered = emb[block(k), :].astype(jnp.float32) - mean_values
        half = centered.astype(jnp.bfloat16)
        cen[block(k), :] = half
        half = half.astype(jnp.float32)
        squares[0, pl.ds((j + k) % N, 1), :] = jnp.sum(centered * centered, 0, keepdims=True)
        squares[1, pl.ds((j + k) % N, 1), :] = jnp.sum(half * half, 0, keepdims=True)

    def multiply(k):
        product = product_transposed(cen[block(0), :], cen[block(k), :])
        gram[:, block(k)] = product
        gram_half[:, block(k)] = product.astype(jnp.bfloat16)

    own = (pl.ds(m(16 * x, 16), 16), pl.ds(m(64 + 16 * y, 16), 16))
    early, middle, late = pl.ds(0, EARLY), pl.ds(EARLY, LATE - EARLY), pl.ds(LATE, IMG)

    def scatter(cols):
        group = Group("scatter", gram_half.at[pl.ds(0, 96), cols])
        for d in (2, 1, 3):
            rows = pl.ds(m(16 * ((x + d) % SIDE), 16), 16)
            group.push(gram_half.at[rows, cols], gram_one.at[0, d - 1, :, cols], at_x(d))
            rows = pl.ds(m(64 + 16 * ((y + d) % SIDE), 16), 16)
            group.push(gram_half.at[rows, cols], gram_one.at[1, d - 1, :, cols], at_y(d))
        return group

    def spread(cols, before):
        before.wait_recv()
        group = Group("spread", gram_half.at[pl.ds(0, 96), cols])
        for t in range(2):
            total = gram[own[t], cols]
            for d in range(3):
                total = total + gram_one[t, d, :, cols].astype(jnp.float32)
            gram_sum[t, :, cols] = total.astype(jnp.bfloat16)
        for d in (2, 1, 3):
            group.push(gram_sum.at[0, :, cols], gram_two.at[0, d - 1, :, cols], at_y(d))
            group.push(gram_sum.at[1, :, cols], gram_two.at[1, d - 1, :, cols], at_x(d))
        return group

    def collect(cols, before):
        before.wait_recv()
        group = Group("collect", gram_half.at[pl.ds(0, 96), cols])
        for t in range(2):
            total = gram_sum[t, :, cols].astype(jnp.float32)
            for d in range(3):
                total = total + gram_two[t, d, :, cols].astype(jnp.float32)
            gram_all[own[t], cols] = total.astype(jnp.bfloat16)
        for d in (2, 1, 3):
            ref = gram_all.at[own[0], cols]
            group.push(ref, ref, at_x(d))
            ref = gram_all.at[own[1], cols]
            group.push(ref, ref, at_y(d))
        return group

    def last_one():
        group = Group("last_one", gram_half.at[:, pl.ds(0, 3 * IMG)])
        for d in (2, 1, 3):
            group.push(gram_half.at[low, late], last_part.at[0, d - 1], at_x(d))
            group.push(gram_half.at[high, late], last_part.at[1, d - 1], at_y(d))
        return group

    def last_two(before):
        before.wait_recv()
        group = Group("last_two", gram_half.at[:, pl.ds(0, 3 * IMG)])
        for t, rows in enumerate((low, high)):
            total = gram_half[rows, late].astype(jnp.float32)
            for d in range(3):
                total = total + last_part[t, d].astype(jnp.float32)
            last_sum[t] = total.astype(jnp.bfloat16)
        for d in (2, 1, 3):
            group.push(last_sum.at[0], last_part.at[2, d - 1], at_y(d))
            group.push(last_sum.at[1], last_part.at[3, d - 1], at_x(d))
        return group

    def last_end(before):
        before.wait_recv()
        for t, rows in enumerate((low, high)):
            total = last_sum[t].astype(jnp.float32)
            for d in range(3):
                total = total + last_part[2 + t, d].astype(jnp.float32)
            gram_all[rows, late] = total.astype(jnp.bfloat16)

    for k in (0, 1, 7):
        center(k)
    parts = []

    def in_third():
        for k in (0, 1, 7):
            multiply(k)
        for k in (2, 6):
            center(k)
            multiply(k)
        parts.append(scatter(early))

    gather_step("emb", emb, 3, down, up, in_third)
    for k in (3, 5):
        center(k)
        multiply(k)
    parts.append(scatter(middle))
    parts[0] = spread(early, parts[0])
    last_block.wait_recv()
    center(4)
    multiply(4)
    final = last_one()
    parts[1] = spread(middle, parts[1])
    deviation = jnp.sqrt(
        jnp.sum(squares[0], 0, keepdims=True) / (IMAGES - 1) + variance_epsilon
    )
    dev_out[...] = deviation
    diagonal = jnp.sum(squares[1], 0, keepdims=True)
    parts[0] = collect(early, parts[0])
    final = last_two(final)
    parts[1] = collect(middle, parts[1])
    partner_copy.wait_recv()
    parts[0].wait_recv()
    before_last = pl.ds(0, EARLY)
    covariance_part = jnp.dot(
        gram_all[:, before_last], cen[before_last, :], preferred_element_type=jnp.float32
    )
    part[0] = covariance_part
    last_end(final)
    parts[1].wait_recv()

    coefficient = 4.0 * covariance_weight * LOSS_SCALE / (OUT * (IMAGES - 1)) / (IMAGES - 1)
    hinge_scale = jnp.where(deviation < 1.0, 1.0 / deviation, 0.0) * (
        LOSS_SCALE * variance_weight / (2.0 * OUT * (IMAGES - 1))
    )
    direct_scale = LOSS_SCALE * 2.0 * invariance_weight / (IMAGES * OUT)

    def gradient(rows):
        rest = pl.ds(EARLY, IMAGES - EARLY)
        covariance = part[0, rows, :] + jnp.dot(
            gram_all[rows, rest], cen[rest, :], preferred_element_type=jnp.float32
        )
        half = cen[rows, :].astype(jnp.float32)
        values = emb[rows, :].astype(jnp.float32)
        total = (
            direct_scale * (values - partner[rows, :].astype(jnp.float32))
            - hinge_scale * (values - mean_values)
            + coefficient * (covariance - half * diagonal)
        )
        grads[rows, :] = total.astype(jnp.bfloat16)

    def gradients(c):
        if c % 2 == 0:
            gradient(pl.ds(ROWS * c, 2 * ROWS))

    down, up = start_gather("grads", grads, gradients)

    def times(ks, cols):
        n = len(ks)
        left = feats[pl.ds(SLOT[ks[0]], n), :, cols].reshape(n * IMG, cols.size)
        right = grads[pl.ds(PLACE[ks[0]] * IMG, n * IMG), :]
        return transposed_product(left, right)

    acc[...] = times((0,), orows)
    mine[...] = times((0,), wrows)
    for step in range(1, 3):
        last_block = gather_step("grads", grads, step, down, up)
        acc[...] += times((step, N - step), orows)
        mine[...] += times((step, N - step), wrows)
    gather_step("grads", grads, 3, down, up)
    acc[...] += times((3, 5), orows)
    last_block.wait_recv()
    lasts = []
    for i in range(2):
        rows = pl.ds(i * 256, 256)
        product = times((4,), pl.ds(m((1 - v) * WIDTH + i * 256, 256), 256))
        give[rows, :] = (acc[rows, :] + product).astype(jnp.bfloat16)
        lasts.append(push("last", give.at[rows], theirs.at[rows], other))
    mine[...] += times((3, 5), wrows) + times((4,), wrows)
    five = pl.ds(1, 5)
    wait_sends("first", feats.at[five, pl.ds(0, 32), pl.ds(0, 256)])
    wait_sends("second", feats.at[five, pl.ds(0, 96), pl.ds(0, 256)])
    wait_sends("third", feats.at[five, pl.ds(0, 96), :])
    wait_sends("near", feats.at[slots((1, 7))])
    wait_sends("weight", weight)
    wait_sends("far", partner)
    for name in ("reduce", "emb", "grads"):
        wait_sends(name, emb.at[pl.ds(0, 6 * IMG)])
    for name in ("emb_far", "grads_far"):
        wait_sends(name, partner)
    wait_sends("shares", sums.at[pl.ds(0, N - 1)])
    wait_sends("partner", partner)
    for name in ("scatter", "spread", "collect"):
        wait_sends(name, gram_half.at[pl.ds(0, 96), pl.ds(0, LATE)])
    for name in ("last_one", "last_two"):
        wait_sends(name, gram_half.at[:, pl.ds(0, 3 * IMG)])
    for i in range(2):
        rows = pl.ds(i * 256, 256)
        lasts[i].wait_recv()
        grad_out[rows, :] = mine[rows, :] + theirs[rows, :].astype(jnp.float32)
    wait_sends("last", give)
    assert not sends and len(groups) <= WAITS


def per_device(hidden, weight):
    vmem = pl.BlockSpec(memory_space=pltpu.VMEM)
    hbm = pl.BlockSpec(memory_space=pltpu.HBM)
    half, full = jnp.bfloat16, jnp.float32
    return pl.pallas_call(
        kernel,
        out_shape=(
            jax.ShapeDtypeStruct((1, IMG, WIDTH), half),
            jax.ShapeDtypeStruct((WIDTH, WIDTH), full),
            jax.ShapeDtypeStruct((1, WIDTH), full),
        ),
        in_specs=[hbm, hbm],
        out_specs=(vmem, vmem, vmem),
        scratch_shapes=[
            pltpu.VMEM((IMG, OUT), half),
            pltpu.VMEM((N, IMG, 2 * WIDTH), half),
            pltpu.VMEM((2 * WIDTH, WIDTH), half),
            pltpu.VMEM((N, IMG, WIDTH), full),
            pltpu.VMEM((2, PARTS, ROWS, 256), half),
            pltpu.VMEM((2, PARTS, ROWS, 256), half),
            pltpu.VMEM((2, 3, PARTS, ROWS, WIDTH), half),
            pltpu.VMEM((2, 3, PARTS, ROWS, WIDTH), half),
            pltpu.VMEM((IMAGES, WIDTH), half),
            pltpu.VMEM((IMAGES, WIDTH), half),
            pltpu.VMEM((IMG, WIDTH), half),
            pltpu.VMEM((N, 1, WIDTH), full),
            pltpu.VMEM((2, N, WIDTH), full),
            pltpu.VMEM((IMG, IMAGES), full),
            pltpu.VMEM((IMG, IMAGES), half),
            pltpu.VMEM((2, 3, 16, IMAGES), half),
            pltpu.VMEM((2, 16, IMAGES), half),
            pltpu.VMEM((2, 3, 16, IMAGES), half),
            pltpu.VMEM((4, 3, 64, IMG), half),
            pltpu.VMEM((2, 64, IMG), half),
            pltpu.VMEM((IMG, IMAGES), half),
            pltpu.VMEM((IMAGES, WIDTH), half),
            pltpu.VMEM((WIDTH, WIDTH), full),
            pltpu.VMEM((WIDTH, WIDTH), full),
            pltpu.VMEM((WIDTH, WIDTH), half),
            pltpu.VMEM((WIDTH, WIDTH), half),
            pltpu.SemaphoreType.DMA((2,)),
            pltpu.SemaphoreType.DMA((SENDS,)),
            pltpu.SemaphoreType.DMA((WAITS,)),
        ],
        compiler_params=pltpu.CompilerParams(
            collective_id=0, has_side_effects=True, vmem_limit_bytes=52 << 20
        ),
        name="expander",
    )(hidden, weight)


def solution(mesh):
    placed = (P("view", "dp", None), P(("view", "dp"), "unit"))
    return jax.shard_map(
        per_device,
        mesh=mesh,
        in_specs=placed,
        out_specs=(P("view", "dp", "unit"), P(("view", "dp"), "unit"), P("view", "unit")),
        check_vma=False,
    )
```

```python
import jax
import jax.numpy as jnp
from jax import lax
from jax.experimental import pallas as pl
from jax.experimental.pallas import tpu as pltpu
from jax.sharding import PartitionSpec as P

invariance_weight = 25.0
variance_weight = 25.0
covariance_weight = 1.0
variance_epsilon = 0.0001

IMG = 128
N = 8
SIDE = 4
WIDTH = 512
OUT = 8192
IMAGES = IMG * N
LOSS_SCALE = IMAGES * OUT / 4096.0
SLOT = {0: 0, 4: 1, 3: 2, 5: 3, 2: 4, 6: 5, 1: 6, 7: 7}
PLACE = {0: 0, 1: 1, 7: 2, 2: 3, 6: 4, 3: 5, 5: 6, 4: 7}
GROUPS = ((4,), (3, 5), (2, 6))
EARLY, LATE = 5 * IMG, 7 * IMG
PARTS = 4
ROWS = IMG // PARTS
WAITS = 104
SENDS = 19


def transposed_product(left, right):
    return lax.dot_general(
        left, right, (((0,), (0,)), ((), ())), preferred_element_type=jnp.float32
    )


def product_transposed(left, right):
    return lax.dot_general(
        left, right, (((1,), (1,)), ((), ())), preferred_element_type=jnp.float32
    )


def kernel(
    hidden,
    weight,
    emb_out,
    grad_out,
    dev_out,
    held,
    feats,
    wgt,
    part,
    far_send,
    far_recv,
    red_send,
    red_recv,
    emb,
    cen,
    partner,
    sums,
    squares,
    gram,
    gram_half,
    gram_one,
    gram_sum,
    gram_two,
    last_part,
    last_sum,
    gram_all,
    grads,
    acc,
    mine,
    give,
    theirs,
    local_sem,
    send_sem,
    recv_sem,
):
    v, j, u = lax.axis_index("view"), lax.axis_index("dp"), lax.axis_index("unit")
    x, y = u // SIDE, u % SIDE

    def at_z(k):
        return (v, (j + k + N) % N, u)

    def at_x(d):
        return (v, j, ((x + d) % SIDE) * SIDE + y)

    def at_y(d):
        return (v, j, x * SIDE + (y + d) % SIDE)

    other = (1 - v, j, u)
    groups, sends = [], {}

    class Group:
        def __init__(self, name, like):
            self.at, self.name, self.like = len(groups), name, like
            groups.append(self)
            sends.setdefault(name, len(sends))

        def push(self, src, dst, device):
            pltpu.make_async_remote_copy(
                src_ref=src,
                dst_ref=dst,
                send_sem=send_sem.at[sends[self.name]],
                recv_sem=recv_sem.at[self.at],
                device_id=device,
                device_id_type=pl.DeviceIdType.MESH,
            ).start()

        def wait_recv(self):
            pltpu.make_async_copy(self.like, self.like, recv_sem.at[self.at]).wait()

    def push(name, src, dst, device):
        group = Group(name, src)
        group.push(src, dst, device)
        return group

    def wait_sends(name, like):
        pltpu.make_async_copy(like, like, send_sem.at[sends.pop(name)]).wait()

    def m(value, by):
        return pl.multiple_of(value, by)

    def slots(group):
        return pl.ds(SLOT[group[0]], len(group))

    wrows = pl.ds(m(v * WIDTH, WIDTH), WIDTH)
    orows = pl.ds(m((1 - v) * WIDTH, WIDTH), WIDTH)
    load_hidden = pltpu.make_async_copy(hidden.at[0], held, local_sem.at[0])
    load_weight = pltpu.make_async_copy(weight, wgt.at[wrows], local_sem.at[1])
    load_hidden.start()
    load_weight.start()

    def columns_of(block, c):
        return pl.ds(m(c * (OUT // 2) + block * WIDTH, WIDTH), WIDTH)

    barrier = pltpu.get_barrier_semaphore()
    peers = [at_z(k) for k in range(1, N)]
    peers += [at_x(d) for d in range(1, SIDE)] + [at_y(d) for d in range(1, SIDE)] + [other]
    for peer in peers:
        pl.semaphore_signal(barrier, inc=1, device_id=peer, device_id_type=pl.DeviceIdType.MESH)
    pl.semaphore_wait(barrier, len(peers))

    a_rows, a_cols = pl.ds(m(16 * y, 16), 16), pl.ds(m(256 * x, 256), 256)
    b_rows, b_cols = pl.ds(m(64 + 16 * x, 16), 16), pl.ds(m(256 * y, 256), 256)
    load_hidden.wait()
    first = []
    for group in GROUPS:
        first.append(Group("first", feats.at[slots(group), pl.ds(0, 32), pl.ds(0, 256)]))
        for k in group:
            to = (j - k + N) % N
            a_from = pl.ds(m((x // 2) * (OUT // 2) + to * WIDTH + (x % 2) * 256, 256), 256)
            b_from = pl.ds(m((y // 2) * (OUT // 2) + to * WIDTH + (y % 2) * 256, 256), 256)
            a_to, b_to = feats.at[SLOT[k], a_rows, a_cols], feats.at[SLOT[k], b_rows, b_cols]
            first[-1].push(held.at[a_rows, a_from], a_to, at_z(-k))
            first[-1].push(held.at[b_rows, b_from], b_to, at_z(-k))
        if group == (4,):
            load_weight.wait()
            weight_copy = push("weight", wgt.at[wrows], wgt.at[wrows], other)

    def project(k):
        part[SLOT[k]] = jnp.dot(feats[SLOT[k]], wgt[...], preferred_element_type=jnp.float32)


    second, third = [], []

    def along_one(g):
        group = GROUPS[g]
        first[g].wait_recv()
        a = feats.at[slots(group), a_rows, a_cols]
        b = feats.at[slots(group), b_rows, b_cols]
        second.append(Group("second", feats.at[slots(group), pl.ds(0, 96), pl.ds(0, 256)]))
        for d in (2, 1, 3):
            second[g].push(a, a, at_x(d))
            second[g].push(b, b, at_y(d))

    def along_both(g):
        group = GROUPS[g]
        second[g].wait_recv()
        a = feats.at[slots(group), a_rows, :]
        b = feats.at[slots(group), b_rows, :]
        third.append(Group("third", feats.at[slots(group), pl.ds(0, 96), :]))
        for d in (2, 1, 3):
            third[g].push(a, a, at_y(d))
            third[g].push(b, b, at_x(d))

    def take(g):
        third[g].wait_recv()

    low, high = pl.ds(0, 64), pl.ds(64, 64)

    def reduce_far(way, c):
        rows, cols = pl.ds(ROWS * c, ROWS), pl.ds(256 * way, 256)
        far_send[way, c] = part[SLOT[4], rows, cols].astype(jnp.bfloat16)
        return push(
            "far", far_send.at[way, c], far_recv.at[way, c], at_z(-2 if way == 0 else 2)
        )

    def reduce_on(way, step, k, c, before=None, far=None):
        rows, cols = pl.ds(ROWS * c, ROWS), pl.ds(256 * way, 256)
        total = part[SLOT[k], rows, :]
        if before is not None:
            before.wait_recv()
            total = total + red_recv[way, step - 1, c].astype(jnp.float32)
        red_send[way, step, c] = total.astype(jnp.bfloat16)
        if far is not None:
            far.wait_recv()
            total = total[:, 256 * way : 256 * way + 256]
            total = total + far_recv[way, c].astype(jnp.float32)
            red_send[way, step, c, :, cols] = total.astype(jnp.bfloat16)
        return push(
            "reduce",
            red_send.at[way, step, c],
            red_recv.at[way, step, c],
            at_z(-1 if way == 0 else 1),
        )

    along_one(0)
    along_one(1)
    near = Group("near", feats.at[slots((1, 7))])
    for c in range(2):
        for k in (1, 7):
            to = (j - k + N) % N
            at = feats.at[SLOT[k], :, pl.ds(c * WIDTH, WIDTH)]
            near.push(held.at[:, columns_of(to, c)], at, at_z(-k))
    along_one(2)
    along_both(0)
    along_both(1)
    for c in range(2):
        feats[0, :, pl.ds(c * WIDTH, WIDTH)] = held[:, columns_of(j, c)]
    weight_copy.wait_recv()
    project(0)
    take(0)
    project(4)
    far = [[reduce_far(way, c) for way in range(2)] for c in range(PARTS)]
    along_both(2)
    take(1)
    running = [[None, None] for c in range(PARTS)]
    for step in range(3):
        for way, k in ((0, 5 + step), (1, 3 - step)):
            if step == 0:
                project(k)
                running[0][way] = reduce_on(way, 0, k, 0)
        for c in range(PARTS):
            for way, k in ((0, 5 + step), (1, 3 - step)):
                if step == 0 and c == 0:
                    continue
                running[c][way] = reduce_on(
                    way, step, k, c, running[c][way], far[c][way] if step == 1 else None
                )
        if step == 0:
            near.wait_recv()
            project(7)
            project(1)
            take(2)
            project(6)
            project(2)

    def finish(c):
        rows = pl.ds(ROWS * c, ROWS)
        total = part[0, rows, :] + (
            red_recv[0, 2, c].astype(jnp.float32) + red_recv[1, 2, c].astype(jnp.float32)
        )
        emb[rows, :] = total.astype(jnp.bfloat16)

    def block(k):
        return pl.ds(PLACE[k] * IMG, IMG)

    def chunk(k, c):
        return pl.ds(PLACE[k] * IMG + ROWS * c, ROWS)

    def start_gather(name, buf, make):
        down, up = [], []
        for c in range(PARTS):
            make(c)
            down.append(push(name, buf.at[chunk(0, c)], buf.at[chunk(1, c)], at_z(-1)))
            up.append(push(name, buf.at[chunk(0, c)], buf.at[chunk(7, c)], at_z(1)))
        return down, up

    def gather_step(name, buf, step, down, up, between=None):
        far = None
        if step == 2:
            far = Group(name + "_far", buf.at[pl.ds(0, IMG)])
        for h in range(PARTS):
            for ways, way, at, to in ((down, 0, step, step + 1), (up, 1, N - step, N - step - 1)):
                ways[h].wait_recv()
                if step < 3:
                    ways[h] = push(
                        name,
                        buf.at[chunk(at, h)],
                        buf.at[chunk(to, h)],
                        at_z(-1 if way == 0 else 1),
                    )
                if step == 2:
                    for i in (h,):
                        cols = pl.ds(256 * way, 256)
                        far.push(
                            buf.at[chunk(at, i), cols],
                            buf.at[chunk(4, i), cols],
                            at_z(-2 if way == 0 else 2),
                        )
            if h == 0 and between is not None:
                between()
        return far

    def reduced(c):
        for way in range(2):
            running[c][way].wait_recv()
        finish(c)

    down, up = start_gather("emb", emb, reduced)
    sums[pl.ds(j, 1)] = jnp.sum(emb[block(0), :].astype(jnp.float32), 0, keepdims=True)[None]
    shares = Group("shares", sums.at[pl.ds(0, N - 1)])
    for k in (4, 3, 5, 2, 6, 1, 7):
        shares.push(sums.at[pl.ds(j, 1)], sums.at[pl.ds(j, 1)], at_z(k))
    partner_copy = push("partner", emb.at[block(0)], partner, other)
    emb_out[0] = emb[block(0), :]

    gather_step("emb", emb, 1, down, up)
    last_block = gather_step("emb", emb, 2, down, up)
    shares.wait_recv()
    mean_values = jnp.sum(sums[...], 0) / IMAGES

    def center(k):
        centered = emb[block(k), :].astype(jnp.float32) - mean_values
        half = centered.astype(jnp.bfloat16)
        cen[block(k), :] = half
        half = half.astype(jnp.float32)
        squares[0, pl.ds((j + k) % N, 1), :] = jnp.sum(centered * centered, 0, keepdims=True)
        squares[1, pl.ds((j + k) % N, 1), :] = jnp.sum(half * half, 0, keepdims=True)

    def multiply(k):
        product = product_transposed(cen[block(0), :], cen[block(k), :])
        gram[:, block(k)] = product
        gram_half[:, block(k)] = product.astype(jnp.bfloat16)

    own = (pl.ds(m(16 * x, 16), 16), pl.ds(m(64 + 16 * y, 16), 16))
    early, middle, late = pl.ds(0, EARLY), pl.ds(EARLY, LATE - EARLY), pl.ds(LATE, IMG)

    def scatter(cols):
        group = Group("scatter", gram_half.at[pl.ds(0, 96), cols])
        for d in (2, 1, 3):
            rows = pl.ds(m(16 * ((x + d) % SIDE), 16), 16)
            group.push(gram_half.at[rows, cols], gram_one.at[0, d - 1, :, cols], at_x(d))
            rows = pl.ds(m(64 + 16 * ((y + d) % SIDE), 16), 16)
            group.push(gram_half.at[rows, cols], gram_one.at[1, d - 1, :, cols], at_y(d))
        return group

    def spread(cols, before):
        before.wait_recv()
        group = Group("spread", gram_half.at[pl.ds(0, 96), cols])
        for t in range(2):
            total = gram[own[t], cols]
            for d in range(3):
                total = total + gram_one[t, d, :, cols].astype(jnp.float32)
            gram_sum[t, :, cols] = total.astype(jnp.bfloat16)
        for d in (2, 1, 3):
            group.push(gram_sum.at[0, :, cols], gram_two.at[0, d - 1, :, cols], at_y(d))
            group.push(gram_sum.at[1, :, cols], gram_two.at[1, d - 1, :, cols], at_x(d))
        return group

    def collect(cols, before):
        before.wait_recv()
        group = Group("collect", gram_half.at[pl.ds(0, 96), cols])
        for t in range(2):
            total = gram_sum[t, :, cols].astype(jnp.float32)
            for d in range(3):
                total = total + gram_two[t, d, :, cols].astype(jnp.float32)
            gram_all[own[t], cols] = total.astype(jnp.bfloat16)
        for d in (2, 1, 3):
            ref = gram_all.at[own[0], cols]
            group.push(ref, ref, at_x(d))
            ref = gram_all.at[own[1], cols]
            group.push(ref, ref, at_y(d))
        return group

    def inner(cols):
        return pl.ds(cols.start - EARLY, cols.size)

    def last_one(cols):
        group = Group("last_one", gram_half.at[:, pl.ds(0, 3 * cols.size)])
        for d in (2, 1, 3):
            group.push(gram_half.at[low, cols], last_part.at[0, d - 1, :, inner(cols)], at_x(d))
            group.push(gram_half.at[high, cols], last_part.at[1, d - 1, :, inner(cols)], at_y(d))
        return group

    def last_two(cols, before):
        before.wait_recv()
        group = Group("last_two", gram_half.at[:, pl.ds(0, 3 * cols.size)])
        at = inner(cols)
        for t, rows in enumerate((low, high)):
            total = gram_half[rows, cols].astype(jnp.float32)
            for d in range(3):
                total = total + last_part[t, d, :, at].astype(jnp.float32)
            last_sum[t, :, at] = total.astype(jnp.bfloat16)
        for d in (2, 1, 3):
            group.push(last_sum.at[0, :, at], last_part.at[2, d - 1, :, at], at_y(d))
            group.push(last_sum.at[1, :, at], last_part.at[3, d - 1, :, at], at_x(d))
        return group

    def last_end(cols, before):
        before.wait_recv()
        at = inner(cols)
        for t, rows in enumerate((low, high)):
            total = last_sum[t, :, at].astype(jnp.float32)
            for d in range(3):
                total = total + last_part[2 + t, d, :, at].astype(jnp.float32)
            gram_all[rows, cols] = total.astype(jnp.bfloat16)

    for k in (0, 1, 7):
        center(k)
    parts = []

    def in_third():
        for k in (0, 1, 7):
            multiply(k)
        for k in (2, 6):
            center(k)
            multiply(k)
        parts.append(scatter(early))

    gather_step("emb", emb, 3, down, up, in_third)
    for k in (3, 5):
        center(k)
        multiply(k)
    between = last_one(middle)
    parts[0] = spread(early, parts[0])
    last_block.wait_recv()
    center(4)
    multiply(4)
    final = last_one(late)
    between = last_two(middle, between)
    deviation = jnp.sqrt(
        jnp.sum(squares[0], 0, keepdims=True) / (IMAGES - 1) + variance_epsilon
    )
    dev_out[...] = deviation
    diagonal = jnp.sum(squares[1], 0, keepdims=True)
    parts[0] = collect(early, parts[0])
    final = last_two(late, final)
    last_end(middle, between)
    partner_copy.wait_recv()
    parts[0].wait_recv()
    before_last = pl.ds(0, EARLY)
    covariance_part = jnp.dot(
        gram_all[:, before_last], cen[before_last, :], preferred_element_type=jnp.float32
    )
    part[0] = covariance_part
    last_end(late, final)

    coefficient = 4.0 * covariance_weight * LOSS_SCALE / (OUT * (IMAGES - 1)) / (IMAGES - 1)
    hinge_scale = jnp.where(deviation < 1.0, 1.0 / deviation, 0.0) * (
        LOSS_SCALE * variance_weight / (2.0 * OUT * (IMAGES - 1))
    )
    direct_scale = LOSS_SCALE * 2.0 * invariance_weight / (IMAGES * OUT)

    def gradient(rows):
        rest = pl.ds(EARLY, IMAGES - EARLY)
        covariance = part[0, rows, :] + jnp.dot(
            gram_all[rows, rest], cen[rest, :], preferred_element_type=jnp.float32
        )
        half = cen[rows, :].astype(jnp.float32)
        values = emb[rows, :].astype(jnp.float32)
        total = (
            direct_scale * (values - partner[rows, :].astype(jnp.float32))
            - hinge_scale * (values - mean_values)
            + coefficient * (covariance - half * diagonal)
        )
        grads[rows, :] = total.astype(jnp.bfloat16)

    def gradients(c):
        if c % 2 == 0:
            gradient(pl.ds(ROWS * c, 2 * ROWS))

    down, up = start_gather("grads", grads, gradients)

    def times(ks, cols):
        n = len(ks)
        left = feats[pl.ds(SLOT[ks[0]], n), :, cols].reshape(n * IMG, cols.size)
        right = grads[pl.ds(PLACE[ks[0]] * IMG, n * IMG), :]
        return transposed_product(left, right)

    acc[...] = times((0,), orows)
    mine[...] = times((0,), wrows)
    for step in range(1, 3):
        last_block = gather_step("grads", grads, step, down, up)
        acc[...] += times((step, N - step), orows)
        mine[...] += times((step, N - step), wrows)
    gather_step("grads", grads, 3, down, up)
    acc[...] += times((3, 5), orows)
    last_block.wait_recv()
    lasts = []
    for i in range(2):
        rows = pl.ds(i * 256, 256)
        product = times((4,), pl.ds(m((1 - v) * WIDTH + i * 256, 256), 256))
        give[rows, :] = (acc[rows, :] + product).astype(jnp.bfloat16)
        lasts.append(push("last", give.at[rows], theirs.at[rows], other))
    mine[...] += times((3, 5), wrows) + times((4,), wrows)
    five = pl.ds(1, 5)
    wait_sends("first", feats.at[five, pl.ds(0, 32), pl.ds(0, 256)])
    wait_sends("second", feats.at[five, pl.ds(0, 96), pl.ds(0, 256)])
    wait_sends("third", feats.at[five, pl.ds(0, 96), :])
    wait_sends("near", feats.at[slots((1, 7))])
    wait_sends("weight", weight)
    wait_sends("far", partner)
    for name in ("reduce", "emb", "grads"):
        wait_sends(name, emb.at[pl.ds(0, 6 * IMG)])
    for name in ("emb_far", "grads_far"):
        wait_sends(name, partner)
    wait_sends("shares", sums.at[pl.ds(0, N - 1)])
    wait_sends("partner", partner)
    for name in ("scatter", "spread", "collect"):
        wait_sends(name, gram_half.at[pl.ds(0, 96), early])
    for name in ("last_one", "last_two"):
        wait_sends(name, emb.at[pl.ds(0, 288)])
    for i in range(2):
        rows = pl.ds(i * 256, 256)
        lasts[i].wait_recv()
        grad_out[rows, :] = mine[rows, :] + theirs[rows, :].astype(jnp.float32)
    wait_sends("last", give)
    assert not sends and len(groups) <= WAITS


def per_device(hidden, weight):
    vmem = pl.BlockSpec(memory_space=pltpu.VMEM)
    hbm = pl.BlockSpec(memory_space=pltpu.HBM)
    half, full = jnp.bfloat16, jnp.float32
    return pl.pallas_call(
        kernel,
        out_shape=(
            jax.ShapeDtypeStruct((1, IMG, WIDTH), half),
            jax.ShapeDtypeStruct((WIDTH, WIDTH), full),
            jax.ShapeDtypeStruct((1, WIDTH), full),
        ),
        in_specs=[hbm, hbm],
        out_specs=(vmem, vmem, vmem),
        scratch_shapes=[
            pltpu.VMEM((IMG, OUT), half),
            pltpu.VMEM((N, IMG, 2 * WIDTH), half),
            pltpu.VMEM((2 * WIDTH, WIDTH), half),
            pltpu.VMEM((N, IMG, WIDTH), full),
            pltpu.VMEM((2, PARTS, ROWS, 256), half),
            pltpu.VMEM((2, PARTS, ROWS, 256), half),
            pltpu.VMEM((2, 3, PARTS, ROWS, WIDTH), half),
            pltpu.VMEM((2, 3, PARTS, ROWS, WIDTH), half),
            pltpu.VMEM((IMAGES, WIDTH), half),
            pltpu.VMEM((IMAGES, WIDTH), half),
            pltpu.VMEM((IMG, WIDTH), half),
            pltpu.VMEM((N, 1, WIDTH), full),
            pltpu.VMEM((2, N, WIDTH), full),
            pltpu.VMEM((IMG, IMAGES), full),
            pltpu.VMEM((IMG, IMAGES), half),
            pltpu.VMEM((2, 3, 16, IMAGES), half),
            pltpu.VMEM((2, 16, IMAGES), half),
            pltpu.VMEM((2, 3, 16, IMAGES), half),
            pltpu.VMEM((4, 3, 64, 3 * IMG), half),
            pltpu.VMEM((2, 64, 3 * IMG), half),
            pltpu.VMEM((IMG, IMAGES), half),
            pltpu.VMEM((IMAGES, WIDTH), half),
            pltpu.VMEM((WIDTH, WIDTH), full),
            pltpu.VMEM((WIDTH, WIDTH), full),
            pltpu.VMEM((WIDTH, WIDTH), half),
            pltpu.VMEM((WIDTH, WIDTH), half),
            pltpu.SemaphoreType.DMA((2,)),
            pltpu.SemaphoreType.DMA((SENDS,)),
            pltpu.SemaphoreType.DMA((WAITS,)),
        ],
        compiler_params=pltpu.CompilerParams(
            collective_id=0, has_side_effects=True, vmem_limit_bytes=52 << 20
        ),
        name="expander",
    )(hidden, weight)


def solution(mesh):
    placed = (P("view", "dp", None), P(("view", "dp"), "unit"))
    return jax.shard_map(
        per_device,
        mesh=mesh,
        in_specs=placed,
        out_specs=(P("view", "dp", "unit"), P(("view", "dp"), "unit"), P("view", "unit")),
        check_vma=False,
    )
```

```python
import jax
import jax.numpy as jnp
from jax import lax
from jax.experimental import pallas as pl
from jax.experimental.pallas import tpu as pltpu
from jax.sharding import PartitionSpec as P

invariance_weight = 25.0
variance_weight = 25.0
covariance_weight = 1.0
variance_epsilon = 0.0001

IMG = 128
N = 8
SIDE = 4
WIDTH = 512
OUT = 8192
IMAGES = IMG * N
LOSS_SCALE = IMAGES * OUT / 4096.0
SLOT = {0: 0, 4: 1, 3: 2, 5: 3, 2: 4, 6: 5, 1: 6, 7: 7}
PLACE = {0: 0, 1: 1, 7: 2, 2: 3, 6: 4, 3: 5, 5: 6, 4: 7}
GROUPS = ((4,), (3, 5), (2, 6))
EARLY, LATE = 5 * IMG, 7 * IMG
PARTS = 4
ROWS = IMG // PARTS
WAITS = 104
SENDS = 19


def transposed_product(left, right):
    return lax.dot_general(
        left, right, (((0,), (0,)), ((), ())), preferred_element_type=jnp.float32
    )


def product_transposed(left, right):
    return lax.dot_general(
        left, right, (((1,), (1,)), ((), ())), preferred_element_type=jnp.float32
    )


def kernel(
    hidden,
    weight,
    emb_out,
    grad_out,
    dev_out,
    held,
    feats,
    wgt,
    part,
    far_send,
    far_recv,
    red_send,
    red_recv,
    emb,
    cen,
    partner,
    sums,
    squares,
    gram,
    gram_half,
    gram_one,
    gram_sum,
    gram_two,
    last_part,
    last_sum,
    gram_all,
    grads,
    acc,
    mine,
    give,
    theirs,
    local_sem,
    send_sem,
    recv_sem,
):
    v, j, u = lax.axis_index("view"), lax.axis_index("dp"), lax.axis_index("unit")
    x, y = u // SIDE, u % SIDE

    def at_z(k):
        return (v, (j + k + N) % N, u)

    def at_x(d):
        return (v, j, ((x + d) % SIDE) * SIDE + y)

    def at_y(d):
        return (v, j, x * SIDE + (y + d) % SIDE)

    other = (1 - v, j, u)
    groups, sends = [], {}

    class Group:
        def __init__(self, name, like):
            self.at, self.name, self.like = len(groups), name, like
            groups.append(self)
            sends.setdefault(name, len(sends))

        def push(self, src, dst, device):
            pltpu.make_async_remote_copy(
                src_ref=src,
                dst_ref=dst,
                send_sem=send_sem.at[sends[self.name]],
                recv_sem=recv_sem.at[self.at],
                device_id=device,
                device_id_type=pl.DeviceIdType.MESH,
            ).start()

        def wait_recv(self):
            pltpu.make_async_copy(self.like, self.like, recv_sem.at[self.at]).wait()

    def push(name, src, dst, device):
        group = Group(name, src)
        group.push(src, dst, device)
        return group

    def wait_sends(name, like):
        pltpu.make_async_copy(like, like, send_sem.at[sends.pop(name)]).wait()

    def m(value, by):
        return pl.multiple_of(value, by)

    def slots(group):
        return pl.ds(SLOT[group[0]], len(group))

    wrows = pl.ds(m(v * WIDTH, WIDTH), WIDTH)
    orows = pl.ds(m((1 - v) * WIDTH, WIDTH), WIDTH)
    load_hidden = pltpu.make_async_copy(hidden.at[0], held, local_sem.at[0])
    load_weight = pltpu.make_async_copy(weight, wgt.at[wrows], local_sem.at[1])
    load_hidden.start()
    load_weight.start()

    def columns_of(block, c):
        return pl.ds(m(c * (OUT // 2) + block * WIDTH, WIDTH), WIDTH)

    barrier = pltpu.get_barrier_semaphore()
    peers = [at_z(k) for k in range(1, N)]
    peers += [at_x(d) for d in range(1, SIDE)] + [at_y(d) for d in range(1, SIDE)] + [other]
    for peer in peers:
        pl.semaphore_signal(barrier, inc=1, device_id=peer, device_id_type=pl.DeviceIdType.MESH)
    pl.semaphore_wait(barrier, len(peers))

    a_rows, a_cols = pl.ds(m(16 * y, 16), 16), pl.ds(m(256 * x, 256), 256)
    b_rows, b_cols = pl.ds(m(64 + 16 * x, 16), 16), pl.ds(m(256 * y, 256), 256)
    load_hidden.wait()
    first = []
    for group in GROUPS:
        first.append(Group("first", feats.at[slots(group), pl.ds(0, 32), pl.ds(0, 256)]))
        for k in group:
            to = (j - k + N) % N
            a_from = pl.ds(m((x // 2) * (OUT // 2) + to * WIDTH + (x % 2) * 256, 256), 256)
            b_from = pl.ds(m((y // 2) * (OUT // 2) + to * WIDTH + (y % 2) * 256, 256), 256)
            a_to, b_to = feats.at[SLOT[k], a_rows, a_cols], feats.at[SLOT[k], b_rows, b_cols]
            first[-1].push(held.at[a_rows, a_from], a_to, at_z(-k))
            first[-1].push(held.at[b_rows, b_from], b_to, at_z(-k))
        if group == (4,):
            load_weight.wait()
            weight_copy = push("weight", wgt.at[wrows], wgt.at[wrows], other)

    def project(k):
        part[SLOT[k]] = jnp.dot(feats[SLOT[k]], wgt[...], preferred_element_type=jnp.float32)


    second, third = [], []

    def along_one(g):
        group = GROUPS[g]
        first[g].wait_recv()
        a = feats.at[slots(group), a_rows, a_cols]
        b = feats.at[slots(group), b_rows, b_cols]
        second.append(Group("second", feats.at[slots(group), pl.ds(0, 96), pl.ds(0, 256)]))
        for d in (2, 1, 3):
            second[g].push(a, a, at_x(d))
            second[g].push(b, b, at_y(d))

    def along_both(g):
        group = GROUPS[g]
        second[g].wait_recv()
        a = feats.at[slots(group), a_rows, :]
        b = feats.at[slots(group), b_rows, :]
        third.append(Group("third", feats.at[slots(group), pl.ds(0, 96), :]))
        for d in (2, 1, 3):
            third[g].push(a, a, at_y(d))
            third[g].push(b, b, at_x(d))

    def take(g):
        third[g].wait_recv()

    low, high = pl.ds(0, 64), pl.ds(64, 64)

    def reduce_far(way, c):
        rows, cols = pl.ds(ROWS * c, ROWS), pl.ds(256 * way, 256)
        far_send[way, c] = part[SLOT[4], rows, cols].astype(jnp.bfloat16)
        return push(
            "far", far_send.at[way, c], far_recv.at[way, c], at_z(-2 if way == 0 else 2)
        )

    def reduce_on(way, step, k, c, before=None, far=None):
        rows, cols = pl.ds(ROWS * c, ROWS), pl.ds(256 * way, 256)
        total = part[SLOT[k], rows, :]
        if before is not None:
            before.wait_recv()
            total = total + red_recv[way, step - 1, c].astype(jnp.float32)
        red_send[way, step, c] = total.astype(jnp.bfloat16)
        if far is not None:
            far.wait_recv()
            total = total[:, 256 * way : 256 * way + 256]
            total = total + far_recv[way, c].astype(jnp.float32)
            red_send[way, step, c, :, cols] = total.astype(jnp.bfloat16)
        return push(
            "reduce",
            red_send.at[way, step, c],
            red_recv.at[way, step, c],
            at_z(-1 if way == 0 else 1),
        )

    along_one(0)
    along_one(1)
    near = Group("near", feats.at[slots((1, 7))])
    for c in range(2):
        for k in (1, 7):
            to = (j - k + N) % N
            at = feats.at[SLOT[k], :, pl.ds(c * WIDTH, WIDTH)]
            near.push(held.at[:, columns_of(to, c)], at, at_z(-k))
    along_one(2)
    along_both(0)
    along_both(1)
    for c in range(2):
        feats[0, :, pl.ds(c * WIDTH, WIDTH)] = held[:, columns_of(j, c)]
    weight_copy.wait_recv()
    project(0)
    take(0)
    project(4)
    far = [[reduce_far(way, c) for way in range(2)] for c in range(PARTS)]
    along_both(2)
    take(1)
    running = [[None, None] for c in range(PARTS)]
    for step in range(3):
        for way, k in ((0, 5 + step), (1, 3 - step)):
            if step == 0:
                project(k)
                running[0][way] = reduce_on(way, 0, k, 0)
        for c in range(PARTS):
            for way, k in ((0, 5 + step), (1, 3 - step)):
                if step == 0 and c == 0:
                    continue
                running[c][way] = reduce_on(
                    way, step, k, c, running[c][way], far[c][way] if step == 1 else None
                )
        if step == 0:
            near.wait_recv()
            project(7)
            project(1)
            take(2)
            project(6)
            project(2)

    def finish(c):
        rows = pl.ds(ROWS * c, ROWS)
        total = part[0, rows, :] + (
            red_recv[0, 2, c].astype(jnp.float32) + red_recv[1, 2, c].astype(jnp.float32)
        )
        emb[rows, :] = total.astype(jnp.bfloat16)

    def block(k):
        return pl.ds(PLACE[k] * IMG, IMG)

    def chunk(k, c):
        return pl.ds(PLACE[k] * IMG + ROWS * c, ROWS)

    def start_gather(name, buf, make):
        down, up = [], []
        for c in range(PARTS):
            make(c)
            down.append(push(name, buf.at[chunk(0, c)], buf.at[chunk(1, c)], at_z(-1)))
            up.append(push(name, buf.at[chunk(0, c)], buf.at[chunk(7, c)], at_z(1)))
        return down, up

    def gather_step(name, buf, step, down, up, between=None):
        far = None
        if step == 2:
            far = Group(name + "_far", buf.at[pl.ds(0, IMG)])
        for h in range(PARTS):
            for ways, way, at, to in ((down, 0, step, step + 1), (up, 1, N - step, N - step - 1)):
                ways[h].wait_recv()
                if step < 3:
                    ways[h] = push(
                        name,
                        buf.at[chunk(at, h)],
                        buf.at[chunk(to, h)],
                        at_z(-1 if way == 0 else 1),
                    )
                if step == 2:
                    for i in (h,):
                        cols = pl.ds(256 * way, 256)
                        far.push(
                            buf.at[chunk(at, i), cols],
                            buf.at[chunk(4, i), cols],
                            at_z(-2 if way == 0 else 2),
                        )
            if h == 0 and between is not None:
                between()
        return far

    def reduced(c):
        for way in range(2):
            running[c][way].wait_recv()
        finish(c)

    down, up = start_gather("emb", emb, reduced)
    sums[pl.ds(j, 1)] = jnp.sum(emb[block(0), :].astype(jnp.float32), 0, keepdims=True)[None]
    shares = Group("shares", sums.at[pl.ds(0, N - 1)])
    for k in (4, 3, 5, 2, 6, 1, 7):
        shares.push(sums.at[pl.ds(j, 1)], sums.at[pl.ds(j, 1)], at_z(k))
    partner_copy = push("partner", emb.at[block(0)], partner, other)
    emb_out[0] = emb[block(0), :]

    gather_step("emb", emb, 1, down, up)
    last_block = gather_step("emb", emb, 2, down, up)
    shares.wait_recv()
    mean_values = jnp.sum(sums[...], 0) / IMAGES

    def center(k):
        centered = emb[block(k), :].astype(jnp.float32) - mean_values
        half = centered.astype(jnp.bfloat16)
        cen[block(k), :] = half
        half = half.astype(jnp.float32)
        squares[0, pl.ds((j + k) % N, 1), :] = jnp.sum(centered * centered, 0, keepdims=True)
        squares[1, pl.ds((j + k) % N, 1), :] = jnp.sum(half * half, 0, keepdims=True)

    def multiply(k):
        product = product_transposed(cen[block(0), :], cen[block(k), :])
        gram[:, block(k)] = product
        gram_half[:, block(k)] = product.astype(jnp.bfloat16)

    own = (pl.ds(m(16 * x, 16), 16), pl.ds(m(64 + 16 * y, 16), 16))
    early, middle, late = pl.ds(0, EARLY), pl.ds(EARLY, LATE - EARLY), pl.ds(LATE, IMG)

    def scatter(cols):
        group = Group("scatter", gram_half.at[pl.ds(0, 96), cols])
        for d in (2, 1, 3):
            rows = pl.ds(m(16 * ((x + d) % SIDE), 16), 16)
            group.push(gram_half.at[rows, cols], gram_one.at[0, d - 1, :, cols], at_x(d))
            rows = pl.ds(m(64 + 16 * ((y + d) % SIDE), 16), 16)
            group.push(gram_half.at[rows, cols], gram_one.at[1, d - 1, :, cols], at_y(d))
        return group

    def spread(cols, before):
        before.wait_recv()
        group = Group("spread", gram_half.at[pl.ds(0, 96), cols])
        for t in range(2):
            total = gram[own[t], cols]
            for d in range(3):
                total = total + gram_one[t, d, :, cols].astype(jnp.float32)
            gram_sum[t, :, cols] = total.astype(jnp.bfloat16)
        for d in (2, 1, 3):
            group.push(gram_sum.at[0, :, cols], gram_two.at[0, d - 1, :, cols], at_y(d))
            group.push(gram_sum.at[1, :, cols], gram_two.at[1, d - 1, :, cols], at_x(d))
        return group

    def collect(cols, before):
        before.wait_recv()
        group = Group("collect", gram_half.at[pl.ds(0, 96), cols])
        for t in range(2):
            total = gram_sum[t, :, cols].astype(jnp.float32)
            for d in range(3):
                total = total + gram_two[t, d, :, cols].astype(jnp.float32)
            gram_all[own[t], cols] = total.astype(jnp.bfloat16)
        for d in (2, 1, 3):
            ref = gram_all.at[own[0], cols]
            group.push(ref, ref, at_x(d))
            ref = gram_all.at[own[1], cols]
            group.push(ref, ref, at_y(d))
        return group

    def inner(cols):
        return pl.ds(cols.start - EARLY, cols.size)

    def last_one(cols):
        group = Group("last_one", gram_half.at[:, pl.ds(0, 3 * cols.size)])
        for d in (2, 1, 3):
            group.push(gram_half.at[low, cols], last_part.at[0, d - 1, :, inner(cols)], at_x(d))
            group.push(gram_half.at[high, cols], last_part.at[1, d - 1, :, inner(cols)], at_y(d))
        return group

    def last_two(cols, before):
        before.wait_recv()
        group = Group("last_two", gram_half.at[:, pl.ds(0, 3 * cols.size)])
        at = inner(cols)
        for t, rows in enumerate((low, high)):
            total = gram_half[rows, cols].astype(jnp.float32)
            for d in range(3):
                total = total + last_part[t, d, :, at].astype(jnp.float32)
            last_sum[t, :, at] = total.astype(jnp.bfloat16)
        for d in (2, 1, 3):
            group.push(last_sum.at[0, :, at], last_part.at[2, d - 1, :, at], at_y(d))
            group.push(last_sum.at[1, :, at], last_part.at[3, d - 1, :, at], at_x(d))
        return group

    def last_end(cols, before):
        before.wait_recv()
        at = inner(cols)
        for t, rows in enumerate((low, high)):
            total = last_sum[t, :, at].astype(jnp.float32)
            for d in range(3):
                total = total + last_part[2 + t, d, :, at].astype(jnp.float32)
            gram_all[rows, cols] = total.astype(jnp.bfloat16)

    for k in (0, 1, 7):
        center(k)
    parts = []

    def in_third():
        for k in (0, 1, 7):
            multiply(k)
        for k in (2, 6):
            center(k)
            multiply(k)
        parts.append(scatter(early))

    in_third()
    gather_step("emb", emb, 3, down, up)
    for k in (3, 5):
        center(k)
        multiply(k)
    between = last_one(middle)
    parts[0] = spread(early, parts[0])
    last_block.wait_recv()
    center(4)
    multiply(4)
    final = last_one(late)
    between = last_two(middle, between)
    deviation = jnp.sqrt(
        jnp.sum(squares[0], 0, keepdims=True) / (IMAGES - 1) + variance_epsilon
    )
    dev_out[...] = deviation
    diagonal = jnp.sum(squares[1], 0, keepdims=True)
    parts[0] = collect(early, parts[0])
    final = last_two(late, final)
    last_end(middle, between)
    partner_copy.wait_recv()
    parts[0].wait_recv()
    before_last = pl.ds(0, EARLY)
    covariance_part = jnp.dot(
        gram_all[:, before_last], cen[before_last, :], preferred_element_type=jnp.float32
    )
    part[0] = covariance_part
    last_end(late, final)

    coefficient = 4.0 * covariance_weight * LOSS_SCALE / (OUT * (IMAGES - 1)) / (IMAGES - 1)
    hinge_scale = jnp.where(deviation < 1.0, 1.0 / deviation, 0.0) * (
        LOSS_SCALE * variance_weight / (2.0 * OUT * (IMAGES - 1))
    )
    direct_scale = LOSS_SCALE * 2.0 * invariance_weight / (IMAGES * OUT)

    def gradient(rows):
        rest = pl.ds(EARLY, IMAGES - EARLY)
        covariance = part[0, rows, :] + jnp.dot(
            gram_all[rows, rest], cen[rest, :], preferred_element_type=jnp.float32
        )
        half = cen[rows, :].astype(jnp.float32)
        values = emb[rows, :].astype(jnp.float32)
        total = (
            direct_scale * (values - partner[rows, :].astype(jnp.float32))
            - hinge_scale * (values - mean_values)
            + coefficient * (covariance - half * diagonal)
        )
        grads[rows, :] = total.astype(jnp.bfloat16)

    def gradients(c):
        if c % 2 == 0:
            gradient(pl.ds(ROWS * c, 2 * ROWS))

    down, up = start_gather("grads", grads, gradients)

    def times(ks, cols):
        n = len(ks)
        left = feats[pl.ds(SLOT[ks[0]], n), :, cols].reshape(n * IMG, cols.size)
        right = grads[pl.ds(PLACE[ks[0]] * IMG, n * IMG), :]
        return transposed_product(left, right)

    acc[...] = times((0,), orows)
    mine[...] = times((0,), wrows)
    for step in range(1, 3):
        last_block = gather_step("grads", grads, step, down, up)
        acc[...] += times((step, N - step), orows)
        mine[...] += times((step, N - step), wrows)
    gather_step("grads", grads, 3, down, up)
    acc[...] += times((3, 5), orows)
    last_block.wait_recv()
    lasts = []
    for i in range(2):
        rows = pl.ds(i * 256, 256)
        product = times((4,), pl.ds(m((1 - v) * WIDTH + i * 256, 256), 256))
        give[rows, :] = (acc[rows, :] + product).astype(jnp.bfloat16)
        lasts.append(push("last", give.at[rows], theirs.at[rows], other))
    mine[...] += times((3, 5), wrows) + times((4,), wrows)
    five = pl.ds(1, 5)
    wait_sends("first", feats.at[five, pl.ds(0, 32), pl.ds(0, 256)])
    wait_sends("second", feats.at[five, pl.ds(0, 96), pl.ds(0, 256)])
    wait_sends("third", feats.at[five, pl.ds(0, 96), :])
    wait_sends("near", feats.at[slots((1, 7))])
    wait_sends("weight", weight)
    wait_sends("far", partner)
    for name in ("reduce", "emb", "grads"):
        wait_sends(name, emb.at[pl.ds(0, 6 * IMG)])
    for name in ("emb_far", "grads_far"):
        wait_sends(name, partner)
    wait_sends("shares", sums.at[pl.ds(0, N - 1)])
    wait_sends("partner", partner)
    for name in ("scatter", "spread", "collect"):
        wait_sends(name, gram_half.at[pl.ds(0, 96), early])
    for name in ("last_one", "last_two"):
        wait_sends(name, emb.at[pl.ds(0, 288)])
    for i in range(2):
        rows = pl.ds(i * 256, 256)
        lasts[i].wait_recv()
        grad_out[rows, :] = mine[rows, :] + theirs[rows, :].astype(jnp.float32)
    wait_sends("last", give)
    assert not sends and len(groups) <= WAITS


def per_device(hidden, weight):
    vmem = pl.BlockSpec(memory_space=pltpu.VMEM)
    hbm = pl.BlockSpec(memory_space=pltpu.HBM)
    half, full = jnp.bfloat16, jnp.float32
    return pl.pallas_call(
        kernel,
        out_shape=(
            jax.ShapeDtypeStruct((1, IMG, WIDTH), half),
            jax.ShapeDtypeStruct((WIDTH, WIDTH), full),
            jax.ShapeDtypeStruct((1, WIDTH), full),
        ),
        in_specs=[hbm, hbm],
        out_specs=(vmem, vmem, vmem),
        scratch_shapes=[
            pltpu.VMEM((IMG, OUT), half),
            pltpu.VMEM((N, IMG, 2 * WIDTH), half),
            pltpu.VMEM((2 * WIDTH, WIDTH), half),
            pltpu.VMEM((N, IMG, WIDTH), full),
            pltpu.VMEM((2, PARTS, ROWS, 256), half),
            pltpu.VMEM((2, PARTS, ROWS, 256), half),
            pltpu.VMEM((2, 3, PARTS, ROWS, WIDTH), half),
            pltpu.VMEM((2, 3, PARTS, ROWS, WIDTH), half),
            pltpu.VMEM((IMAGES, WIDTH), half),
            pltpu.VMEM((IMAGES, WIDTH), half),
            pltpu.VMEM((IMG, WIDTH), half),
            pltpu.VMEM((N, 1, WIDTH), full),
            pltpu.VMEM((2, N, WIDTH), full),
            pltpu.VMEM((IMG, IMAGES), full),
            pltpu.VMEM((IMG, IMAGES), half),
            pltpu.VMEM((2, 3, 16, IMAGES), half),
            pltpu.VMEM((2, 16, IMAGES), half),
            pltpu.VMEM((2, 3, 16, IMAGES), half),
            pltpu.VMEM((4, 3, 64, 3 * IMG), half),
            pltpu.VMEM((2, 64, 3 * IMG), half),
            pltpu.VMEM((IMG, IMAGES), half),
            pltpu.VMEM((IMAGES, WIDTH), half),
            pltpu.VMEM((WIDTH, WIDTH), full),
            pltpu.VMEM((WIDTH, WIDTH), full),
            pltpu.VMEM((WIDTH, WIDTH), half),
            pltpu.VMEM((WIDTH, WIDTH), half),
            pltpu.SemaphoreType.DMA((2,)),
            pltpu.SemaphoreType.DMA((SENDS,)),
            pltpu.SemaphoreType.DMA((WAITS,)),
        ],
        compiler_params=pltpu.CompilerParams(
            collective_id=0, has_side_effects=True, vmem_limit_bytes=52 << 20
        ),
        name="expander",
    )(hidden, weight)


def solution(mesh):
    placed = (P("view", "dp", None), P(("view", "dp"), "unit"))
    return jax.shard_map(
        per_device,
        mesh=mesh,
        in_specs=placed,
        out_specs=(P("view", "dp", "unit"), P(("view", "dp"), "unit"), P("view", "unit")),
        check_vma=False,
    )
```
